32 devices in a mesh: parts: 1, dp: 2 (over core), group: 16 (over z, y, x).
Axes of the slice: x: 2, y: 2, z: 4, core: 2. Of those that a mesh axis runs over, the one named last changes fastest.
Arguments:
- hidden_in: bfloat16 [4, 256, 2048], P(('parts', 'dp'), 'group'), may hold values from -6 to 6
- span_lengths: int32 [4], P('parts'), may hold values from 0 to 256, as said below
- norm_gain: bfloat16 [2048], replicated, may hold values from 0.099609375 to 1.8984375
- query_weight: bfloat16 [2048, 2048], P(None, 'group'), may hold values from -8 to 8
- key_weight: bfloat16 [2048, 256], P(None, 'group'), may hold values from -0.5 to 0.5
- value_weight: bfloat16 [2048, 256], P(None, 'group'), may hold values from -0.125 to 0.125
- out_weight: bfloat16 [2048, 2048], P('group'), may hold values from -0.5 to 0.5
Outputs:
- hidden_out: bfloat16 [4, 256, 2048], P(('parts', 'dp'), 'group')
The draws below stay inside these ranges and needn't reach their ends.
Inputs may be any that keep to these rules, and one draw needn't show every extreme that they name: `span_lengths`: live spans (length above 0) are the leading slots of a dp index; in each part one dp index holds 2 live spans and the other none; the first live span is full.
All inputs are finite; a program needn't handle non-finite values.
Results may differ from the reference program's by a relative error of at most 0.0068.
Values may be sent and summed in bfloat16 or wider, within the bound.
A program may use at most 64 MiB of HBM per device.

```python
import math
import jax
import jax.numpy as jnp
from jax import lax

HD = 128
GQA = 8
SPAN = 256
SLOTS = 2
HEADS = 16
KV_HEADS = 2
D = 2048
N_DP = 2


def key_matrix(key):
    return jax.random.normal(jax.random.fold_in(key, 101), (D, KV_HEADS * HD), jnp.float32) / math.sqrt(D)


def draw_key_weight(key, part):
    shared = key_matrix(key)
    return shared.astype(jnp.bfloat16)


def draw_query_weight(key, part):
    key = jax.random.fold_in(key, 5)
    noise = jax.random.normal(key, (D, HEADS * HD), jnp.float32) / math.sqrt(D)
    return noise.astype(jnp.bfloat16)


def draw_span_lengths(key, part):
    key = jax.random.fold_in(key, 7)
    busy = jax.random.randint(jax.random.fold_in(key, 1), (), 0, N_DP)
    tail = jax.random.randint(jax.random.fold_in(key, 2), (SLOTS,), SPAN // 8, SPAN + 1)
    lengths = jnp.where(jnp.arange(SLOTS) == 0, SPAN, tail)
    holder = jnp.arange(N_DP)[:, None] == busy
    return jnp.where(holder, lengths[None, :], 0).reshape(N_DP * SLOTS).astype(jnp.int32)


def level_of(own_key, shape, cuts, smallest, high):
    level = 1.0
    for axis_at, shards_of in cuts:
        heights = jax.random.uniform(jax.random.fold_in(jax.random.fold_in(own_key, 6), axis_at), (shards_of,), jnp.float32, smallest / len(cuts), high / len(cuts))
        level = level * jnp.repeat(jnp.exp(heights), shape[axis_at] // shards_of).reshape((-1,) + (1,) * (len(shape) - 1 - axis_at))
    return level


def centred(rng, dims, deviation, bound, pieces=(), kind=jnp.bfloat16):
    loudness = level_of(rng, dims, pieces, -0.22, 0.18) if pieces else 1.0
    entries = jax.random.normal(rng, dims, jnp.float32) * deviation * loudness
    return jnp.minimum(jnp.maximum(entries, -bound), bound).astype(kind)


def setup_inputs(seed: int = 0, part: int = 0) -> dict:
    key_list = jax.random.split(jax.random.key(seed), 8)
    part_keys = jax.random.split(jax.random.fold_in(key_list[7], part), 8)
    hidden_in = centred(part_keys[0], (N_DP * SLOTS, SPAN, D), 1.0, 6.0, ((0, 2), (1, 16)))
    span_lengths = draw_span_lengths(jax.random.fold_in(jax.random.fold_in(key_list[7], part), 71), part)
    norm_gain = jnp.clip(1.0 + 0.18 * jax.random.normal(key_list[2], (D,), jnp.float32), 0.099609375, 1.8984375).astype(jnp.bfloat16)
    query_weight = draw_query_weight(jax.random.fold_in(key_list[7], 71), part)
    key_weight = draw_key_weight(jax.random.fold_in(key_list[7], 71), part)
    value_weight = centred(key_list[5], (D, KV_HEADS * HD), D ** -0.5, 0.125, ((1, 16),))
    out_weight = centred(key_list[6], (HEADS * HD, D), HD ** -0.5, 0.5, ((0, 16),))
    return {"hidden_in": hidden_in, "span_lengths": span_lengths, "norm_gain": norm_gain, "query_weight": query_weight, "key_weight": key_weight, "value_weight": value_weight, "out_weight": out_weight}


def rms_rows(rows, gain):
    wide = rows.astype(jnp.float32)
    scale = lax.rsqrt(lax.optimization_barrier(jnp.mean(wide * wide, axis=-1, keepdims=True)) + 1e-05)
    return (wide * scale * gain.astype(jnp.float32)).astype(jnp.bfloat16)

def rotate(block):
    count = block.shape[-2]
    width = block.shape[-1]
    half = width // 2
    positions = jnp.arange(count, dtype=jnp.float32)
    freqs = jnp.exp(-math.log(500000.0) * 2.0 * jnp.arange(half, dtype=jnp.float32) / width)
    angles = positions[:, None] * freqs[None, :]
    cosine = jnp.cos(angles)
    sine = jnp.sin(angles)
    first = block[..., :half]
    second = block[..., half:]
    return jnp.concatenate([first * cosine - second * sine, second * cosine + first * sine], axis=-1)

def reference(hidden_in, span_lengths, norm_gain, query_weight, key_weight, value_weight, out_weight):

    def one_span(pair):
        rows, length = pair
        count = rows.shape[0]
        normed = rms_rows(rows, norm_gain)
        query = jnp.dot(normed, query_weight, preferred_element_type=jnp.float32).astype(jnp.bfloat16)
        keys = jnp.dot(normed, key_weight, preferred_element_type=jnp.float32).astype(jnp.bfloat16)
        values = jnp.dot(normed, value_weight, preferred_element_type=jnp.float32).astype(jnp.bfloat16)
        query = jnp.transpose(query.reshape(count, HEADS, HD), (1, 0, 2))
        keys = jnp.transpose(keys.reshape(count, KV_HEADS, HD), (1, 0, 2))
        values = jnp.transpose(values.reshape(count, KV_HEADS, HD), (1, 0, 2))
        query = rotate(query.astype(jnp.float32)).astype(jnp.bfloat16)
        keys = rotate(keys.astype(jnp.float32)).astype(jnp.bfloat16)
        keys = jnp.repeat(keys, GQA, axis=0)
        values = jnp.repeat(values, GQA, axis=0)
        scores = jnp.einsum('hqd,hkd->hqk', query.astype(jnp.float32), keys.astype(jnp.float32)) / math.sqrt(HD)
        qpos = jnp.arange(count, dtype=jnp.int32)[:, None]
        kpos = jnp.arange(count, dtype=jnp.int32)[None, :]
        allowed = kpos <= qpos
        scores = jnp.where(allowed[None], scores, -1e+30)
        peak = lax.optimization_barrier(jnp.max(scores, axis=-1, keepdims=True))
        expo = jnp.exp(scores - peak)
        weights = (expo / lax.optimization_barrier(jnp.sum(expo, axis=-1, keepdims=True))).astype(jnp.bfloat16)
        heads_out = jnp.einsum('hqk,hkd->hqd', weights.astype(jnp.float32), values.astype(jnp.float32)).astype(jnp.bfloat16)
        heads_out = jnp.transpose(heads_out, (1, 0, 2)).reshape(count, HEADS * HD)
        mixed = jnp.dot(heads_out, out_weight, preferred_element_type=jnp.float32)
        live = jnp.arange(count, dtype=jnp.int32)[:, None] < length
        return jnp.where(live, rows.astype(jnp.float32) + mixed, 0.0).astype(jnp.bfloat16)
    return lax.map(one_span, (hidden_in, span_lengths))
```

```python
import math

import jax
import jax.numpy as jnp
import numpy as np
from jax import lax
from jax.experimental import pallas as pl
from jax.experimental.pallas import tpu as pltpu
from jax.sharding import PartitionSpec as P

MESH = pl.DeviceIdType.MESH


def partner_2(block, axis, stride):
    count = lax.axis_size(axis)
    route = []
    for low in range(count):
        high = low | 1 << stride
        if high != low and high < count:
            route += [(low, high), (high, low)]
    return lax.ppermute(block, axis, route)


def rms_rows(rows, gain):
    wide = rows.astype(jnp.float32)
    scale = lax.rsqrt(jnp.mean(wide * wide, axis=-1, keepdims=True) + 1e-05)
    return (wide * scale * gain.astype(jnp.float32)).astype(jnp.bfloat16)


def rotate(block):
    count = block.shape[-2]
    width = block.shape[-1]
    half = width // 2
    positions = jnp.arange(count, dtype=jnp.float32)
    freqs = jnp.exp(-math.log(500000.0) * 2.0 * jnp.arange(half, dtype=jnp.float32) / width)
    angles = positions[:, None] * freqs[None, :]
    cosine = jnp.cos(angles)
    sine = jnp.sin(angles)
    first = block[..., :half]
    second = block[..., half:]
    return jnp.concatenate(
        [first * cosine - second * sine, second * cosine + first * sine], axis=-1
    )


def attend(span_rows, lengths, norm_gain, query_weight, key_weight, value_weight, out_weight):
    count, rows, width = span_rows.shape
    groups = lax.axis_size("group")
    span = rows * groups
    head_size = query_weight.shape[1]
    key_cols = key_weight.shape[1]
    normed = rms_rows(span_rows, norm_gain)
    joined = jnp.concatenate([query_weight, key_weight, value_weight], axis=1)
    projected = jnp.einsum(
        "prd,dc->prc",
        lax.all_gather(normed, "group", axis=1, tiled=True),
        joined,
        preferred_element_type=jnp.float32,
    ).astype(jnp.bfloat16)
    query = rotate(projected[..., :head_size].astype(jnp.float32)).astype(jnp.bfloat16)
    key_stack = jnp.swapaxes(projected[..., head_size : head_size + key_cols], 1, 2)
    value_stack = jnp.swapaxes(projected[..., head_size + key_cols :], 1, 2)
    my_index = lax.axis_index("group")
    levels = (head_size // key_cols).bit_length() - 1
    for level in range(levels):
        partner = partner_2((key_stack, value_stack), "group", level)
        first_half = my_index // (1 << level) % 2 == 0
        key_stack = jnp.where(
            first_half,
            jnp.concatenate([key_stack, partner[0]], axis=1),
            jnp.concatenate([partner[0], key_stack], axis=1),
        )
        value_stack = jnp.where(
            first_half,
            jnp.concatenate([value_stack, partner[1]], axis=1),
            jnp.concatenate([partner[1], value_stack], axis=1),
        )
    keys = rotate(jnp.swapaxes(key_stack, 1, 2).astype(jnp.float32)).astype(jnp.bfloat16)
    scores = jnp.einsum(
        "pqd,pkd->pqk", query, keys, preferred_element_type=jnp.float32
    ) / math.sqrt(head_size)
    qpos = jnp.arange(span, dtype=jnp.int32)[None, :, None]
    kpos = jnp.arange(span, dtype=jnp.int32)[None, None, :]
    allowed = kpos <= qpos
    scores = jnp.where(allowed, scores, -1e30)
    peak = jnp.max(scores, axis=-1, keepdims=True)
    expo = jnp.exp(scores - peak)
    weights = (expo / jnp.sum(expo, axis=-1, keepdims=True)).astype(jnp.bfloat16)
    heads_out = jnp.einsum(
        "pqk,pdk->pqd", weights, value_stack, preferred_element_type=jnp.float32
    ).astype(jnp.bfloat16)
    head_rows = jnp.swapaxes(heads_out, 0, 1).reshape(span * count, head_size)
    mixed = lax.psum_scatter(
        jnp.dot(head_rows, out_weight, preferred_element_type=jnp.float32),
        "group",
        scatter_dimension=0,
        tiled=True,
    )
    mixed = jnp.swapaxes(mixed.reshape(rows, count, width), 0, 1)
    row_ids = my_index * rows + jnp.arange(rows, dtype=jnp.int32)
    live = row_ids[None, :] < lengths[:, None]
    return jnp.where(live[..., None], span_rows.astype(jnp.float32) + mixed, 0.0).astype(
        jnp.bfloat16
    )


def slot_positions(count):
    at = np.arange(count)
    return (at // 16 % 4) * 64 + (at // 64) * 16 + at % 16


def tables(span, width):
    half = width // 2
    freqs = 500000.0 ** (-2.0 * np.arange(half) / width)
    angles = slot_positions(span)[:, None] * freqs[None, :]
    cosine, sine = np.cos(angles), np.sin(angles)
    wide_cos = np.concatenate([cosine, cosine], axis=1).astype(np.float32)
    wide_sin = np.concatenate([-sine, sine], axis=1).astype(np.float32)
    return wide_cos, wide_sin, cosine.T.astype(np.float32), sine.T.astype(np.float32)


SWAP, GZ, GX, GY, GD, KV, RD, RX, RY, RZ, BACK, COUNT = 0, 1, 5, 9, 13, 17, 33, 37, 41, 45, 49, 50


def span_kernel(
    lens, hidden, gain, wq, wk, wv, wo, cosq, sinq, cosk, sink, out,
    swap_buf, own_rows, x, wqv, wkn, wvn, wov, q, kv, heads, part, out_send, rd, rx, ry, rz, fin, fin_in,
    send, recv, local,
):
    d = lax.axis_index("dp")
    g = lax.axis_index("group")
    z, c = g // 4, g % 4
    zs = (z, z + 1 - 2 * (z % 2), (z + 2) % 4, 3 - z)
    cs = (c, c + 1 - 2 * (c % 2), (c + 2) % 4, 3 - c)

    def chip(zk, ck):
        return {"group": zs[zk] * 4 + cs[ck]}

    near_x, near_y = chip(0, 1), chip(0, 2)
    sibling = {"dp": 1 - d}
    kv_peers = [(k // 4, k % 4) for k in range(1, 8)]
    greeted = [sibling] + [chip(*peer) for peer in kv_peers] + [chip(2, 0), chip(3, 0)]

    loads = [
        pltpu.make_async_copy(wk, wkn, local.at[0]),
        pltpu.make_async_copy(wv, wvn, local.at[1]),
        pltpu.make_async_copy(wq, wqv, local.at[2]),
        pltpu.make_async_copy(wo, wov, local.at[3]),
    ]
    for load in loads:
        load.start()

    barrier = pltpu.get_barrier_semaphore()
    for device in greeted:
        pl.semaphore_signal(barrier, inc=1, device_id=device, device_id_type=MESH)
    pl.semaphore_wait(barrier, len(greeted))

    started = []

    def push(source, target, sent, received, device):
        copy = pltpu.make_async_remote_copy(
            src_ref=source, dst_ref=target, send_sem=send.at[sent], recv_sem=recv.at[received],
            device_id=device, device_id_type=MESH,
        )
        copy.start()
        started.append(copy)

    def take(target, received):
        pltpu.make_async_remote_copy(
            src_ref=target, dst_ref=target, send_sem=send.at[received], recv_sem=recv.at[received],
            device_id=sibling, device_id_type=MESH,
        ).wait_recv()

    push(hidden.at[1 - d], swap_buf, SWAP, SWAP, sibling)
    busy = jnp.where(lens[0] > 0, 0, 1)
    length = jnp.where(busy == 0, lens[d], lens[2 + d])
    take(swap_buf, SWAP)
    rows = jnp.where(busy == d, hidden[d].astype(jnp.float32), swap_buf[...].astype(jnp.float32))
    own_rows[...] = rows
    scale = lax.rsqrt(jnp.mean(rows * rows, axis=-1, keepdims=True) + 1e-05)

    def slot(ck, zk):
        return cs[ck] * 4 + zs[zk]

    def block(ck, zk):
        return x.at[slot(ck, zk)]

    x[slot(0, 0)] = (rows * scale * gain[...].astype(jnp.float32)).astype(jnp.bfloat16)

    def spread(k):
        push(block(0, k), block(0, k), GX + k, GX + k, near_x)
        push(block(0, k), block(0, k), GY + k, GY + k, near_y)

    for k in (1, 2, 3):
        push(block(0, 0), block(0, 0), GZ + k, GZ + k, chip(k, 0))
    spread(0)

    def relay(k):
        if k % 2 == 0:
            take(block(1, k), GX + k)
            push(block(1, k), block(1, k), GD + k, GD + k, near_y)
        else:
            take(block(2, k), GY + k)
            push(block(2, k), block(2, k), GD + k, GD + k, near_x)

    take(block(0, 1), GZ + 1)
    spread(1)
    relay(0)
    take(block(0, 2), GZ + 2)
    spread(2)
    relay(1)
    take(block(0, 3), GZ + 3)
    spread(3)
    relay(2)
    relay(3)

    for load in loads:
        load.wait()

    member = g % 8

    def project(half):
        lines = x[pl.ds(half * 8, 8)].reshape(128, x.shape[2])
        q[pl.ds(half * 128, 128), :] = jnp.dot(lines, wqv[...], preferred_element_type=jnp.float32).astype(jnp.bfloat16)
        keys = jnp.dot(lines, wkn[...], preferred_element_type=jnp.float32)
        values = jnp.dot(lines, wvn[...], preferred_element_type=jnp.float32)
        kv[half, member, 0:16, :] = keys.T.astype(jnp.bfloat16)
        kv[half, member, 16:32, :] = values.T.astype(jnp.bfloat16)
        for k, peer in enumerate(kv_peers, 1):
            index = KV + half * 8 + k
            push(kv.at[half, member], kv.at[half, member], index, index, chip(*peer))

    first = c // 2
    take(block(1, 1), GX + 1)
    take(block(1, 3), GX + 3)
    project(first)
    take(block(2, 0), GY)
    take(block(2, 2), GY + 2)
    for k in range(4):
        take(block(3, k), GD + k)
    project(1 - first)

    wide = q[...].astype(jnp.float32)
    query = (wide * cosq[...] + pltpu.roll(wide, 64, 1) * sinq[...]).astype(jnp.bfloat16)
    for half in range(2):
        for k, (zk, ck) in enumerate(kv_peers, 1):
            take(kv.at[half, (zs[zk] % 2) * 4 + cs[ck]], KV + half * 8 + k)

    def joined(low):
        return jnp.concatenate([kv[half, :, low : low + 16, :].reshape(128, 128) for half in range(2)], axis=1)

    keys = joined(0).astype(jnp.float32)
    upper, lower = keys[:64], keys[64:]
    turned = jnp.concatenate(
        [upper * cosk[...] - lower * sink[...], lower * cosk[...] + upper * sink[...]], axis=0
    ).astype(jnp.bfloat16)
    scores = jnp.dot(query, turned, preferred_element_type=jnp.float32) * (1.0 / math.sqrt(128))

    def position(dim):
        at = lax.broadcasted_iota(jnp.int32, scores.shape, dim)
        return ((at >> 4) & 3) * 64 + (at >> 6) * 16 + (at & 15)

    scores = jnp.where(position(1) <= position(0), scores, -1e30)
    expo = jnp.exp(scores - jnp.max(scores, axis=-1, keepdims=True))
    weights = (expo / jnp.sum(expo, axis=-1, keepdims=True)).astype(jnp.bfloat16)
    heads[...] = lax.dot_general(
        weights, joined(16), (((1,), (1,)), ((), ())), preferred_element_type=jnp.float32
    ).astype(jnp.bfloat16)

    def partial(ck):
        mine = heads[pl.ds(cs[ck] * 64, 64), :]
        return jnp.dot(mine, wov[...], preferred_element_type=jnp.float32).reshape(4, 16, wov.shape[1])

    out_send[pl.ds(cs[3] * 4, 4)] = partial(3).astype(jnp.bfloat16)
    for k in (2, 3, 0, 1):
        push(out_send.at[slot(3, k)], rd.at[k], RD + k, RD + k, near_x if k % 2 == 0 else near_y)
    part[pl.ds(cs[1] * 4, 4)] = partial(1)
    part[pl.ds(cs[2] * 4, 4)] = partial(2)

    def hand_on(ck, k, with_relayed):
        own = part[slot(ck, k)]
        if with_relayed:
            take(rd.at[k], RD + k)
            own = own + rd[k].astype(jnp.float32)
        out_send[slot(ck, k)] = own.astype(jnp.bfloat16)
        if ck == 1:
            push(out_send.at[slot(1, k)], rx.at[k], RX + k, RX + k, near_x)
        else:
            push(out_send.at[slot(2, k)], ry.at[k], RY + k, RY + k, near_y)

    for k in (2, 3, 0, 1):
        hand_on(1 if k % 2 == 0 else 2, k, False)
    part[pl.ds(cs[0] * 4, 4)] = partial(0)
    for k in (2, 3, 0, 1):
        hand_on(2 if k % 2 == 0 else 1, k, True)

    def column_sum(k):
        take(rx.at[k], RX + k)
        take(ry.at[k], RY + k)
        return part[slot(0, k)] + rx[k].astype(jnp.float32) + ry[k].astype(jnp.float32)

    for k in (2, 3, 1):
        out_send[slot(0, k)] = column_sum(k).astype(jnp.bfloat16)
        push(out_send.at[slot(0, k)], rz.at[k], RZ + k, RZ + k, chip(k, 0))
    total = column_sum(0)
    for k in (2, 3, 1):
        take(rz.at[k], RZ + k)
        total = total + rz[k].astype(jnp.float32)
    ids = g * 16 + lax.broadcasted_iota(jnp.int32, total.shape, 0)
    fin[...] = jnp.where(ids < length, own_rows[...] + total, 0.0).astype(jnp.bfloat16)
    push(fin, fin_in, BACK, BACK, sibling)
    out[d] = fin[...]
    take(fin_in, BACK)
    out[1 - d] = fin_in[...]
    for copy in started:
        copy.wait_send()


def fused(hidden_in, span_lengths, norm_gain, query_weight, key_weight, value_weight, out_weight):
    slots, rows, width = hidden_in.shape
    head_size = query_weight.shape[1]
    span = rows * 16
    vmem = pl.BlockSpec(memory_space=pltpu.VMEM)
    anywhere = pl.BlockSpec(memory_space=pl.ANY)
    bf16, f32 = jnp.bfloat16, jnp.float32
    result = pl.pallas_call(
        span_kernel,
        out_shape=jax.ShapeDtypeStruct(hidden_in.shape, bf16),
        in_specs=[pl.BlockSpec(memory_space=pltpu.SMEM), vmem, vmem] + [anywhere] * 4 + [vmem] * 4,
        out_specs=vmem,
        scratch_shapes=[
            pltpu.VMEM((rows, width), bf16),
            pltpu.VMEM((rows, width), f32),
            pltpu.VMEM((16, rows, width), bf16),
            pltpu.VMEM(query_weight.shape, bf16),
            pltpu.VMEM(key_weight.shape, bf16),
            pltpu.VMEM(value_weight.shape, bf16),
            pltpu.VMEM(out_weight.shape, bf16),
            pltpu.VMEM((span, head_size), bf16),
            pltpu.VMEM((2, 8, 32, 128), bf16),
            pltpu.VMEM((span, head_size), bf16),
            pltpu.VMEM((16, rows, width), f32),
            pltpu.VMEM((16, rows, width), bf16),
            pltpu.VMEM((4, rows, width), bf16),
            pltpu.VMEM((4, rows, width), bf16),
            pltpu.VMEM((4, rows, width), bf16),
            pltpu.VMEM((4, rows, width), bf16),
            pltpu.VMEM((rows, width), bf16),
            pltpu.VMEM((rows, width), bf16),
            pltpu.SemaphoreType.DMA((COUNT,)),
            pltpu.SemaphoreType.DMA((COUNT,)),
            pltpu.SemaphoreType.DMA((4,)),
        ],
        compiler_params=pltpu.CompilerParams(
            collective_id=0, has_side_effects=True, vmem_limit_bytes=32 * 1024 * 1024
        ),
        cost_estimate=pl.CostEstimate(
            flops=4 * span * width * head_size, bytes_accessed=4 * width * head_size, transcendentals=span * span
        ),
    )(
        span_lengths, hidden_in, norm_gain.reshape(1, width), query_weight, key_weight, value_weight,
        out_weight, *tables(span, head_size),
    )
    holds = lax.dynamic_index_in_dim(span_lengths, lax.axis_index("dp") * slots, keepdims=False) > 0
    return jnp.where(holds, result, jnp.zeros_like(result))


def shards(hidden_in, span_lengths, norm_gain, query_weight, key_weight, value_weight, out_weight):
    slots = hidden_in.shape[0]
    if (
        lax.axis_size("group") == 16
        and lax.axis_size("dp") == 2
        and hidden_in.shape[:2] == (2, 16)
        and query_weight.shape[1] == 128
        and key_weight.shape[1] == 16
    ):
        return fused(
            hidden_in, span_lengths, norm_gain, query_weight, key_weight, value_weight, out_weight
        )
    dp_index = lax.axis_index("dp")
    own_lengths = lax.dynamic_slice_in_dim(span_lengths, dp_index * slots, slots)
    return attend(
        hidden_in, own_lengths, norm_gain, query_weight, key_weight, value_weight, out_weight
    )


def solution(mesh):
    placed = (
        P(("parts", "dp"), "group", None),
        P("parts"),
        P(),
        P(None, "group"),
        P(None, "group"),
        P(None, "group"),
        P("group", None),
    )
    return jax.shard_map(
        shards,
        mesh=mesh,
        in_specs=placed,
        out_specs=P(("parts", "dp"), "group", None),
        check_vma=False,
    )
```

```python
import math

import jax
import jax.numpy as jnp
import numpy as np
from jax import lax
from jax.experimental import pallas as pl
from jax.experimental.pallas import tpu as pltpu
from jax.sharding import PartitionSpec as P

MESH = pl.DeviceIdType.MESH


def partner_2(block, axis, stride):
    count = lax.axis_size(axis)
    route = []
    for low in range(count):
        high = low | 1 << stride
        if high != low and high < count:
            route += [(low, high), (high, low)]
    return lax.ppermute(block, axis, route)


def rms_rows(rows, gain):
    wide = rows.astype(jnp.float32)
    scale = lax.rsqrt(jnp.mean(wide * wide, axis=-1, keepdims=True) + 1e-05)
    return (wide * scale * gain.astype(jnp.float32)).astype(jnp.bfloat16)


def rotate(block):
    count = block.shape[-2]
    width = block.shape[-1]
    half = width // 2
    positions = jnp.arange(count, dtype=jnp.float32)
    freqs = jnp.exp(-math.log(500000.0) * 2.0 * jnp.arange(half, dtype=jnp.float32) / width)
    angles = positions[:, None] * freqs[None, :]
    cosine = jnp.cos(angles)
    sine = jnp.sin(angles)
    first = block[..., :half]
    second = block[..., half:]
    return jnp.concatenate(
        [first * cosine - second * sine, second * cosine + first * sine], axis=-1
    )


def attend(span_rows, lengths, norm_gain, query_weight, key_weight, value_weight, out_weight):
    count, rows, width = span_rows.shape
    groups = lax.axis_size("group")
    span = rows * groups
    head_size = query_weight.shape[1]
    key_cols = key_weight.shape[1]
    normed = rms_rows(span_rows, norm_gain)
    joined = jnp.concatenate([query_weight, key_weight, value_weight], axis=1)
    projected = jnp.einsum(
        "prd,dc->prc",
        lax.all_gather(normed, "group", axis=1, tiled=True),
        joined,
        preferred_element_type=jnp.float32,
    ).astype(jnp.bfloat16)
    query = rotate(projected[..., :head_size].astype(jnp.float32)).astype(jnp.bfloat16)
    key_stack = jnp.swapaxes(projected[..., head_size : head_size + key_cols], 1, 2)
    value_stack = jnp.swapaxes(projected[..., head_size + key_cols :], 1, 2)
    my_index = lax.axis_index("group")
    levels = (head_size // key_cols).bit_length() - 1
    for level in range(levels):
        partner = partner_2((key_stack, value_stack), "group", level)
        first_half = my_index // (1 << level) % 2 == 0
        key_stack = jnp.where(
            first_half,
            jnp.concatenate([key_stack, partner[0]], axis=1),
            jnp.concatenate([partner[0], key_stack], axis=1),
        )
        value_stack = jnp.where(
            first_half,
            jnp.concatenate([value_stack, partner[1]], axis=1),
            jnp.concatenate([partner[1], value_stack], axis=1),
        )
    keys = rotate(jnp.swapaxes(key_stack, 1, 2).astype(jnp.float32)).astype(jnp.bfloat16)
    scores = jnp.einsum(
        "pqd,pkd->pqk", query, keys, preferred_element_type=jnp.float32
    ) / math.sqrt(head_size)
    qpos = jnp.arange(span, dtype=jnp.int32)[None, :, None]
    kpos = jnp.arange(span, dtype=jnp.int32)[None, None, :]
    allowed = kpos <= qpos
    scores = jnp.where(allowed, scores, -1e30)
    peak = jnp.max(scores, axis=-1, keepdims=True)
    expo = jnp.exp(scores - peak)
    weights = (expo / jnp.sum(expo, axis=-1, keepdims=True)).astype(jnp.bfloat16)
    heads_out = jnp.einsum(
        "pqk,pdk->pqd", weights, value_stack, preferred_element_type=jnp.float32
    ).astype(jnp.bfloat16)
    head_rows = jnp.swapaxes(heads_out, 0, 1).reshape(span * count, head_size)
    mixed = lax.psum_scatter(
        jnp.dot(head_rows, out_weight, preferred_element_type=jnp.float32),
        "group",
        scatter_dimension=0,
        tiled=True,
    )
    mixed = jnp.swapaxes(mixed.reshape(rows, count, width), 0, 1)
    row_ids = my_index * rows + jnp.arange(rows, dtype=jnp.int32)
    live = row_ids[None, :] < lengths[:, None]
    return jnp.where(live[..., None], span_rows.astype(jnp.float32) + mixed, 0.0).astype(
        jnp.bfloat16
    )


def slot_positions(count):
    at = np.arange(count)
    return (at // 16 % 4) * 64 + (at // 64) * 16 + at % 16


def tables(span, width):
    half = width // 2
    freqs = 500000.0 ** (-2.0 * np.arange(half) / width)
    angles = slot_positions(span)[:, None] * freqs[None, :]
    cosine, sine = np.cos(angles), np.sin(angles)
    wide_cos = np.concatenate([cosine, cosine], axis=1).astype(np.float32)
    wide_sin = np.concatenate([-sine, sine], axis=1).astype(np.float32)
    return np.stack([wide_cos, wide_sin]), np.stack([cosine.T, sine.T]).astype(np.float32)


SWAP, GZ, GX, GY, GD, KV, RD, RX, RY, RZ, BACK, COUNT = 0, 1, 5, 9, 13, 17, 33, 37, 41, 45, 49, 50


def span_kernel(
    lens, hidden, gain, wq, wk, wv, wo, wide_table, tall_table, out,
    gain_rows, own_in, swap_buf, own_rows, x, wqv, wkv, wov, turn_q, turn_k, q, kv, heads, part, out_send, rd, rx, ry, rz, fin, fin_in,
    send, recv, local,
):
    d = lax.axis_index("dp")
    g = lax.axis_index("group")
    z, c = g // 4, g % 4
    zs = (z, z + 1 - 2 * (z % 2), (z + 2) % 4, 3 - z)
    cs = (c, c + 1 - 2 * (c % 2), (c + 2) % 4, 3 - c)

    def chip(zk, ck):
        return {"group": zs[zk] * 4 + cs[ck]}

    near_x, near_y = chip(0, 1), chip(0, 2)
    sibling = {"dp": 1 - d}
    kv_peers = [(k // 4, k % 4) for k in range(1, 8)]
    greeted = [sibling] + [chip(*peer) for peer in kv_peers] + [chip(2, 0), chip(3, 0)]

    loads = [
        pltpu.make_async_copy(wk, wkv.at[0:16], local.at[0]),
        pltpu.make_async_copy(wv, wkv.at[16:32], local.at[1]),
        pltpu.make_async_copy(wq, wqv, local.at[2]),
        pltpu.make_async_copy(wo, wov, local.at[3]),
        pltpu.make_async_copy(wide_table, turn_q, local.at[4]),
        pltpu.make_async_copy(tall_table, turn_k, local.at[5]),
    ]
    early = [
        pltpu.make_async_copy(hidden.at[d], own_in, local.at[6]),
        pltpu.make_async_copy(gain, gain_rows, local.at[7]),
    ]
    for load in early + loads:
        load.start()

    barrier = pltpu.get_barrier_semaphore()
    for device in greeted:
        pl.semaphore_signal(barrier, inc=1, device_id=device, device_id_type=MESH)
    pl.semaphore_wait(barrier, len(greeted))

    started = []

    def push(source, target, sent, received, device):
        copy = pltpu.make_async_remote_copy(
            src_ref=source, dst_ref=target, send_sem=send.at[sent], recv_sem=recv.at[received],
            device_id=device, device_id_type=MESH,
        )
        copy.start()
        started.append(copy)

    def take(target, received):
        pltpu.make_async_remote_copy(
            src_ref=target, dst_ref=target, send_sem=send.at[received], recv_sem=recv.at[received],
            device_id=sibling, device_id_type=MESH,
        ).wait_recv()

    push(hidden.at[1 - d], swap_buf, SWAP, SWAP, sibling)
    busy = jnp.where(lens[0] > 0, 0, 1)
    length = jnp.where(busy == 0, lens[d], lens[2 + d])
    for load in early:
        load.wait()
    take(swap_buf, SWAP)
    rows = jnp.where(busy == d, own_in[...].astype(jnp.float32), swap_buf[...].astype(jnp.float32))
    own_rows[...] = rows
    scale = lax.rsqrt(jnp.mean(rows * rows, axis=-1, keepdims=True) + 1e-05)

    def slot(ck, zk):
        return cs[ck] * 4 + zs[zk]

    def block(ck, zk):
        return x.at[slot(ck, zk)]

    x[slot(0, 0)] = (rows * scale * gain_rows[...].astype(jnp.float32)[None, :]).astype(jnp.bfloat16)

    def spread(k):
        push(block(0, k), block(0, k), GX + k, GX + k, near_x)
        push(block(0, k), block(0, k), GY + k, GY + k, near_y)

    for k in (1, 2, 3):
        push(block(0, 0), block(0, 0), GZ + k, GZ + k, chip(k, 0))
    spread(0)

    def relay(k):
        if k % 2 == 0:
            take(block(1, k), GX + k)
            push(block(1, k), block(1, k), GD + k, GD + k, near_y)
        else:
            take(block(2, k), GY + k)
            push(block(2, k), block(2, k), GD + k, GD + k, near_x)

    take(block(0, 1), GZ + 1)
    spread(1)
    relay(0)
    take(block(0, 2), GZ + 2)
    spread(2)
    relay(1)
    take(block(0, 3), GZ + 3)
    spread(3)
    relay(2)
    relay(3)

    for load in loads:
        load.wait()

    member = g % 8

    def project(half):
        lines = x[pl.ds(half * 8, 8)].reshape(128, x.shape[2])
        q[pl.ds(half * 128, 128), :] = jnp.dot(lines, wqv[...], preferred_element_type=jnp.float32).astype(jnp.bfloat16)
        kv[half, member] = lax.dot_general(
            wkv[...], lines, (((1,), (1,)), ((), ())), preferred_element_type=jnp.float32
        ).astype(jnp.bfloat16)
        for k, peer in enumerate(kv_peers, 1):
            index = KV + half * 8 + k
            push(kv.at[half, member], kv.at[half, member], index, index, chip(*peer))

    first = c // 2
    take(block(1, 1), GX + 1)
    take(block(1, 3), GX + 3)
    project(first)
    take(block(2, 0), GY)
    take(block(2, 2), GY + 2)
    for k in range(4):
        take(block(3, k), GD + k)
    project(1 - first)

    wide = q[...].astype(jnp.float32)
    query = (wide * turn_q[0] + pltpu.roll(wide, 64, 1) * turn_q[1]).astype(jnp.bfloat16)
    for half in range(2):
        for k, (zk, ck) in enumerate(kv_peers, 1):
            take(kv.at[half, (zs[zk] % 2) * 4 + cs[ck]], KV + half * 8 + k)

    def joined(low):
        return jnp.concatenate([kv[half, :, low : low + 16, :].reshape(128, 128) for half in range(2)], axis=1)

    keys = joined(0).astype(jnp.float32)
    upper, lower = keys[:64], keys[64:]
    turned = jnp.concatenate(
        [upper * turn_k[0] - lower * turn_k[1], lower * turn_k[0] + upper * turn_k[1]], axis=0
    ).astype(jnp.bfloat16)
    scores = jnp.dot(query, turned, preferred_element_type=jnp.float32) * (1.0 / math.sqrt(128))

    def position(dim):
        at = lax.broadcasted_iota(jnp.int32, scores.shape, dim)
        return ((at >> 4) & 3) * 64 + (at >> 6) * 16 + (at & 15)

    scores = jnp.where(position(1) <= position(0), scores, -1e30)
    expo = jnp.exp(scores - jnp.max(scores, axis=-1, keepdims=True))
    weights = (expo / jnp.sum(expo, axis=-1, keepdims=True)).astype(jnp.bfloat16)
    heads[...] = lax.dot_general(
        weights, joined(16), (((1,), (1,)), ((), ())), preferred_element_type=jnp.float32
    ).astype(jnp.bfloat16)

    def partial(ck):
        mine = heads[pl.ds(cs[ck] * 64, 64), :]
        return jnp.dot(mine, wov[...], preferred_element_type=jnp.float32).reshape(4, 16, wov.shape[1])

    out_send[pl.ds(cs[3] * 4, 4)] = partial(3).astype(jnp.bfloat16)
    for k in (2, 3, 0, 1):
        push(out_send.at[slot(3, k)], rd.at[k], RD + k, RD + k, near_x if k % 2 == 0 else near_y)
    part[pl.ds(cs[1] * 4, 4)] = partial(1)
    part[pl.ds(cs[2] * 4, 4)] = partial(2)

    def hand_on(ck, k, with_relayed):
        own = part[slot(ck, k)]
        if with_relayed:
            take(rd.at[k], RD + k)
            own = own + rd[k].astype(jnp.float32)
        out_send[slot(ck, k)] = own.astype(jnp.bfloat16)
        if ck == 1:
            push(out_send.at[slot(1, k)], rx.at[k], RX + k, RX + k, near_x)
        else:
            push(out_send.at[slot(2, k)], ry.at[k], RY + k, RY + k, near_y)

    for k in (2, 3, 0, 1):
        hand_on(1 if k % 2 == 0 else 2, k, False)
    part[pl.ds(cs[0] * 4, 4)] = partial(0)
    for k in (2, 3, 0, 1):
        hand_on(2 if k % 2 == 0 else 1, k, True)

    def column_sum(k):
        take(rx.at[k], RX + k)
        take(ry.at[k], RY + k)
        return part[slot(0, k)] + rx[k].astype(jnp.float32) + ry[k].astype(jnp.float32)

    for k in (2, 3, 1):
        out_send[slot(0, k)] = column_sum(k).astype(jnp.bfloat16)
        push(out_send.at[slot(0, k)], rz.at[k], RZ + k, RZ + k, chip(k, 0))
    total = column_sum(0)
    for k in (2, 3, 1):
        take(rz.at[k], RZ + k)
        total = total + rz[k].astype(jnp.float32)
    ids = g * 16 + lax.broadcasted_iota(jnp.int32, total.shape, 0)
    fin[...] = jnp.where(ids < length, own_rows[...] + total, 0.0).astype(jnp.bfloat16)
    push(fin, fin_in, BACK, BACK, sibling)
    out[d] = jnp.where(busy == d, fin[...].astype(jnp.float32), 0.0).astype(jnp.bfloat16)
    take(fin_in, BACK)
    out[1 - d] = jnp.where(busy == d, fin_in[...].astype(jnp.float32), 0.0).astype(jnp.bfloat16)
    for copy in started:
        copy.wait_send()


def fused(hidden_in, span_lengths, norm_gain, query_weight, key_weight, value_weight, out_weight):
    _, rows, width = hidden_in.shape
    head_size = query_weight.shape[1]
    span = rows * 16
    vmem = pl.BlockSpec(memory_space=pltpu.VMEM)
    hbm = pl.BlockSpec(memory_space=pltpu.HBM)
    bf16, f32 = jnp.bfloat16, jnp.float32
    wide_table, tall_table = tables(span, head_size)
    return pl.pallas_call(
        span_kernel,
        out_shape=jax.ShapeDtypeStruct(hidden_in.shape, bf16),
        in_specs=[pl.BlockSpec(memory_space=pltpu.SMEM)] + [hbm] * 8,
        out_specs=vmem,
        scratch_shapes=[
            pltpu.VMEM((width,), bf16),
            pltpu.VMEM((rows, width), bf16),
            pltpu.VMEM((rows, width), bf16),
            pltpu.VMEM((rows, width), f32),
            pltpu.VMEM((16, rows, width), bf16),
            pltpu.VMEM(query_weight.shape, bf16),
            pltpu.VMEM((2 * key_weight.shape[1], width), bf16),
            pltpu.VMEM(out_weight.shape, bf16),
            pltpu.VMEM(wide_table.shape, f32),
            pltpu.VMEM(tall_table.shape, f32),
            pltpu.VMEM((span, head_size), bf16),
            pltpu.VMEM((2, 8, 32, 128), bf16),
            pltpu.VMEM((span, head_size), bf16),
            pltpu.VMEM((16, rows, width), f32),
            pltpu.VMEM((16, rows, width), bf16),
            pltpu.VMEM((4, rows, width), bf16),
            pltpu.VMEM((4, rows, width), bf16),
            pltpu.VMEM((4, rows, width), bf16),
            pltpu.VMEM((4, rows, width), bf16),
            pltpu.VMEM((rows, width), bf16),
            pltpu.VMEM((rows, width), bf16),
            pltpu.SemaphoreType.DMA((COUNT,)),
            pltpu.SemaphoreType.DMA((COUNT,)),
            pltpu.SemaphoreType.DMA((8,)),
        ],
        compiler_params=pltpu.CompilerParams(
            collective_id=0, has_side_effects=True, vmem_limit_bytes=56 * 1024 * 1024
        ),
        cost_estimate=pl.CostEstimate(
            flops=4 * span * width * head_size, bytes_accessed=4 * width * head_size, transcendentals=span * span
        ),
    )(
        span_lengths, hidden_in, norm_gain, query_weight, key_weight.T, value_weight.T,
        out_weight, wide_table, tall_table,
    )


def shards(hidden_in, span_lengths, norm_gain, query_weight, key_weight, value_weight, out_weight):
    slots = hidden_in.shape[0]
    if (
        lax.axis_size("group") == 16
        and lax.axis_size("dp") == 2
        and hidden_in.shape[:2] == (2, 16)
        and query_weight.shape[1] == 128
        and key_weight.shape[1] == 16
    ):
        return fused(
            hidden_in, span_lengths, norm_gain, query_weight, key_weight, value_weight, out_weight
        )
    dp_index = lax.axis_index("dp")
    own_lengths = lax.dynamic_slice_in_dim(span_lengths, dp_index * slots, slots)
    return attend(
        hidden_in, own_lengths, norm_gain, query_weight, key_weight, value_weight, out_weight
    )


def solution(mesh):
    placed = (
        P(("parts", "dp"), "group", None),
        P("parts"),
        P(),
        P(None, "group"),
        P(None, "group"),
        P(None, "group"),
        P("group", None),
    )
    return jax.shard_map(
        shards,
        mesh=mesh,
        in_specs=placed,
        out_specs=P(("parts", "dp"), "group", None),
        check_vma=False,
    )
```

```python
import math

import jax
import jax.numpy as jnp
import numpy as np
from jax import lax
from jax.experimental import pallas as pl
from jax.experimental.pallas import tpu as pltpu
from jax.sharding import PartitionSpec as P

MESH = pl.DeviceIdType.MESH


def partner_2(block, axis, stride):
    count = lax.axis_size(axis)
    route = []
    for low in range(count):
        high = low | 1 << stride
        if high != low and high < count:
            route += [(low, high), (high, low)]
    return lax.ppermute(block, axis, route)


def rms_rows(rows, gain):
    wide = rows.astype(jnp.float32)
    scale = lax.rsqrt(jnp.mean(wide * wide, axis=-1, keepdims=True) + 1e-05)
    return (wide * scale * gain.astype(jnp.float32)).astype(jnp.bfloat16)


def rotate(block):
    count = block.shape[-2]
    width = block.shape[-1]
    half = width // 2
    positions = jnp.arange(count, dtype=jnp.float32)
    freqs = jnp.exp(-math.log(500000.0) * 2.0 * jnp.arange(half, dtype=jnp.float32) / width)
    angles = positions[:, None] * freqs[None, :]
    cosine = jnp.cos(angles)
    sine = jnp.sin(angles)
    first = block[..., :half]
    second = block[..., half:]
    return jnp.concatenate(
        [first * cosine - second * sine, second * cosine + first * sine], axis=-1
    )


def attend(span_rows, lengths, norm_gain, query_weight, key_weight, value_weight, out_weight):
    count, rows, width = span_rows.shape
    groups = lax.axis_size("group")
    span = rows * groups
    head_size = query_weight.shape[1]
    key_cols = key_weight.shape[1]
    normed = rms_rows(span_rows, norm_gain)
    joined = jnp.concatenate([query_weight, key_weight, value_weight], axis=1)
    projected = jnp.einsum(
        "prd,dc->prc",
        lax.all_gather(normed, "group", axis=1, tiled=True),
        joined,
        preferred_element_type=jnp.float32,
    ).astype(jnp.bfloat16)
    query = rotate(projected[..., :head_size].astype(jnp.float32)).astype(jnp.bfloat16)
    key_stack = jnp.swapaxes(projected[..., head_size : head_size + key_cols], 1, 2)
    value_stack = jnp.swapaxes(projected[..., head_size + key_cols :], 1, 2)
    my_index = lax.axis_index("group")
    levels = (head_size // key_cols).bit_length() - 1
    for level in range(levels):
        partner = partner_2((key_stack, value_stack), "group", level)
        first_half = my_index // (1 << level) % 2 == 0
        key_stack = jnp.where(
            first_half,
            jnp.concatenate([key_stack, partner[0]], axis=1),
            jnp.concatenate([partner[0], key_stack], axis=1),
        )
        value_stack = jnp.where(
            first_half,
            jnp.concatenate([value_stack, partner[1]], axis=1),
            jnp.concatenate([partner[1], value_stack], axis=1),
        )
    keys = rotate(jnp.swapaxes(key_stack, 1, 2).astype(jnp.float32)).astype(jnp.bfloat16)
    scores = jnp.einsum(
        "pqd,pkd->pqk", query, keys, preferred_element_type=jnp.float32
    ) / math.sqrt(head_size)
    qpos = jnp.arange(span, dtype=jnp.int32)[None, :, None]
    kpos = jnp.arange(span, dtype=jnp.int32)[None, None, :]
    allowed = kpos <= qpos
    scores = jnp.where(allowed, scores, -1e30)
    peak = jnp.max(scores, axis=-1, keepdims=True)
    expo = jnp.exp(scores - peak)
    weights = (expo / jnp.sum(expo, axis=-1, keepdims=True)).astype(jnp.bfloat16)
    heads_out = jnp.einsum(
        "pqk,pdk->pqd", weights, value_stack, preferred_element_type=jnp.float32
    ).astype(jnp.bfloat16)
    head_rows = jnp.swapaxes(heads_out, 0, 1).reshape(span * count, head_size)
    mixed = lax.psum_scatter(
        jnp.dot(head_rows, out_weight, preferred_element_type=jnp.float32),
        "group",
        scatter_dimension=0,
        tiled=True,
    )
    mixed = jnp.swapaxes(mixed.reshape(rows, count, width), 0, 1)
    row_ids = my_index * rows + jnp.arange(rows, dtype=jnp.int32)
    live = row_ids[None, :] < lengths[:, None]
    return jnp.where(live[..., None], span_rows.astype(jnp.float32) + mixed, 0.0).astype(
        jnp.bfloat16
    )


def slot_positions(count):
    at = np.arange(count)
    return (at // 16 % 4) * 64 + (at // 64 % 2) * 32 + (at // 128) * 16 + at % 16


def tables(span, width):
    half = width // 2
    freqs = 500000.0 ** (-2.0 * np.arange(half) / width)
    angles = slot_positions(span)[:, None] * freqs[None, :]
    cosine, sine = np.cos(angles), np.sin(angles)
    wide_cos = np.concatenate([cosine, cosine], axis=1).astype(np.float32)
    wide_sin = np.concatenate([-sine, sine], axis=1).astype(np.float32)
    return np.stack([wide_cos, wide_sin]), np.stack([cosine.T, sine.T]).astype(np.float32)


SWAP, GZ, GY, KV, RY, RZ, BACK, WEIGHT, SHARE, COUNT = 0, 1, 5, 9, 17, 21, 25, 26, 30, 33


def span_kernel(
    lens, hidden, gain, wq, wk, wv, wo, wide_table, tall_table, out,
    gain_rows, own_in, swap_buf, own_rows, x, wqv, wkv, wov, turn_q, turn_k,
    query, kv, heads, part, out_send, ry, rz, fin, fin_in, send, recv, local,
):
    d = lax.axis_index("dp")
    g = lax.axis_index("group")
    z, c = g // 4, g % 4
    y, plane = c // 2, c % 2
    zs = (z, z + 1 - 2 * (z % 2), (z + 2) % 4, 3 - z)
    cs = (c, c + 1 - 2 * (c % 2), (c + 2) % 4, 3 - c)
    wide = x.shape[2]

    def chip(zk, ck):
        return {"group": zs[zk] * 4 + cs[ck]}

    near_x, near_y = chip(0, 1), chip(0, 2)
    sibling = {"dp": 1 - d}
    kv_peers = [(k // 4, k % 4) for k in range(1, 8)]
    greeted = [sibling] + [chip(*peer) for peer in kv_peers] + [chip(2, 0), chip(3, 0)]

    def key_rows(at):
        return wkv.at[pl.ds(at * 32, 16)], wkv.at[pl.ds(at * 32 + 16, 16)]

    def out_rows(at, count=128, low=0):
        return wov.at[pl.ds(at * 128 + low, count)]

    early = [
        pltpu.make_async_copy(hidden.at[d], own_in, local.at[6]),
        pltpu.make_async_copy(gain, gain_rows, local.at[7]),
    ]
    loads = [
        pltpu.make_async_copy(wk, key_rows(plane)[0], local.at[0]),
        pltpu.make_async_copy(wv, key_rows(plane)[1], local.at[1]),
        pltpu.make_async_copy(wq, wqv.at[plane], local.at[2]),
        pltpu.make_async_copy(wo, out_rows(plane), local.at[3]),
        pltpu.make_async_copy(wide_table, turn_q, local.at[4]),
        pltpu.make_async_copy(tall_table, turn_k, local.at[5]),
    ]
    for load in early + loads:
        load.start()

    barrier = pltpu.get_barrier_semaphore()
    for device in greeted:
        pl.semaphore_signal(barrier, inc=1, device_id=device, device_id_type=MESH)
    pl.semaphore_wait(barrier, len(greeted))

    started = []

    def push(source, target, sent, received, device):
        copy = pltpu.make_async_remote_copy(
            src_ref=source, dst_ref=target, send_sem=send.at[sent], recv_sem=recv.at[received],
            device_id=device, device_id_type=MESH,
        )
        copy.start()
        started.append(copy)

    def take(target, received):
        pltpu.make_async_remote_copy(
            src_ref=target, dst_ref=target, send_sem=send.at[received], recv_sem=recv.at[received],
            device_id=sibling, device_id_type=MESH,
        ).wait_recv()

    push(hidden.at[1 - d], swap_buf, SWAP, SWAP, sibling)

    half_q = pl.ds(d * (wide // 2), wide // 2)

    def query_half(at):
        return wqv.at[at, half_q]

    def key_half(at, which):
        return wkv.at[pl.ds(at * 32 + which * 16, 16), half_q]

    def out_half(at):
        return out_rows(at, 64, d * 64)

    push(wq.at[half_q], query_half(plane), WEIGHT, WEIGHT, near_x)
    push(wk.at[:, half_q], key_half(plane, 0), WEIGHT + 1, WEIGHT + 1, near_x)
    push(wv.at[:, half_q], key_half(plane, 1), WEIGHT + 2, WEIGHT + 2, near_x)

    for load in early:
        load.wait()
    busy = jnp.where(lens[0] > 0, 0, 1)
    length = jnp.where(busy == 0, lens[d], lens[2 + d])
    take(swap_buf, SWAP)
    rows = jnp.where(busy == d, own_in[...].astype(jnp.float32), swap_buf[...].astype(jnp.float32))
    own_rows[...] = rows
    scale = lax.rsqrt(jnp.mean(rows * rows, axis=-1, keepdims=True) + 1e-05)

    def slot(yk, zk):
        return (1 - y if yk else y) * 4 + zs[zk]

    def block(yk, zk):
        return x.at[slot(yk, zk)]

    x[slot(0, 0)] = (rows * scale * gain_rows[...].astype(jnp.float32)[None, :]).astype(jnp.bfloat16)

    for k in (3, 2, 1):
        push(block(0, 0), block(0, 0), GZ + k, GZ + k, chip(k, 0))
    push(block(0, 0), block(0, 0), GY, GY, near_y)
    push(wo.at[pl.ds(d * 64, 64)], out_half(plane), WEIGHT + 3, WEIGHT + 3, near_x)
    for k in (1, 2, 3):
        take(block(0, k), GZ + k)
        push(block(0, k), block(0, k), GY + k, GY + k, near_y)

    other = 1 - plane
    take(query_half(other), WEIGHT)
    push(query_half(other), query_half(other), SHARE, SHARE, sibling)
    take(key_half(other, 0), WEIGHT + 1)
    take(key_half(other, 1), WEIGHT + 2)
    both = wkv.at[pl.ds(other * 32, 32), half_q]
    push(both, both, SHARE + 1, SHARE + 1, sibling)
    for load in loads:
        load.wait()
    rest = pl.ds((1 - d) * (wide // 2), wide // 2)
    take(wqv.at[other, rest], SHARE)
    take(wkv.at[pl.ds(other * 32, 32), rest], SHARE + 1)
    for k in range(4):
        take(block(1, k), GY + k)

    lines = x[...].reshape(128, wide)
    pair = (z % 2) * 2 + y
    kv[plane, pl.ds(pair * 2, 2)] = (
        lax.dot_general(wkv[...], lines, (((1,), (1,)), ((), ())), preferred_element_type=jnp.float32)
        .astype(jnp.bfloat16)
        .reshape(2, 32, 128)
    )
    own_kv = kv.at[plane, pl.ds(pair * 2, 2)]
    for k, peer in enumerate(kv_peers, 1):
        push(own_kv, own_kv, KV + k, KV + k, chip(*peer))
    turn = (turn_q[0, pl.ds(plane * 128, 128), :], turn_q[1, pl.ds(plane * 128, 128), :])
    for at in range(2):
        plain = jnp.dot(lines, wqv[at], preferred_element_type=jnp.float32).astype(jnp.bfloat16).astype(jnp.float32)
        query[at * 128 : at * 128 + 128, :] = (plain * turn[0] + pltpu.roll(plain, 64, 1) * turn[1]).astype(jnp.bfloat16)
    take(out_half(other), WEIGHT + 3)
    push(out_half(other), out_half(other), SHARE + 2, SHARE + 2, sibling)
    for k, (zk, ck) in enumerate(kv_peers, 1):
        theirs = (zs[zk] % 2) * 2 + cs[ck] // 2
        take(kv.at[cs[ck] % 2, pl.ds(theirs * 2, 2)], KV + k)

    def joined(low):
        return jnp.concatenate([kv[half, :, low : low + 16, :].reshape(128, 128) for half in range(2)], axis=1)

    keys = joined(0).astype(jnp.float32)
    upper, lower = keys[:64], keys[64:]
    turned = jnp.concatenate(
        [upper * turn_k[0] - lower * turn_k[1], lower * turn_k[0] + upper * turn_k[1]], axis=0
    ).astype(jnp.bfloat16)
    scores = jnp.dot(query[...], turned, preferred_element_type=jnp.float32) * (1.0 / math.sqrt(128))

    def position(dim):
        at = lax.broadcasted_iota(jnp.int32, scores.shape, dim)
        return ((at >> 4) & 3) * 64 + ((at >> 6) & 1) * 32 + (at & 15), at >> 7

    row_at, col_at = position(0)[0] + plane * 16, position(1)[0] + position(1)[1] * 16
    scores = jnp.where(col_at <= row_at, scores, -1e30)
    expo = jnp.exp(scores - jnp.max(scores, axis=-1, keepdims=True))
    weights = (expo / jnp.sum(expo, axis=-1, keepdims=True)).astype(jnp.bfloat16)
    mixed = lax.dot_general(
        weights, joined(16), (((1,), (1,)), ((), ())), preferred_element_type=jnp.float32
    ).astype(jnp.bfloat16)
    heads[:, 0:128] = mixed[0:128]
    heads[:, 128:256] = mixed[128:256]
    take(out_rows(other, 64, (1 - d) * 64), SHARE + 2)

    def partial(at):
        mine = heads[pl.ds(at * 64, 64), :]
        return jnp.dot(mine, wov[...], preferred_element_type=jnp.float32).reshape(4, 16, wide)

    out_send[pl.ds((1 - y) * 4, 4)] = partial(1 - y).astype(jnp.bfloat16)
    for k in (2, 3, 1, 0):
        push(out_send.at[slot(1, k)], ry.at[k], RY + k, RY + k, near_y)
    part[...] = partial(y)

    def column_sum(k):
        take(ry.at[k], RY + k)
        return part[zs[k]] + ry[k].astype(jnp.float32)

    for k in (2, 3, 1):
        out_send[slot(0, k)] = column_sum(k).astype(jnp.bfloat16)
        push(out_send.at[slot(0, k)], rz.at[k], RZ + k, RZ + k, chip(k, 0))
    total = column_sum(0)
    for k in (2, 3, 1):
        take(rz.at[k], RZ + k)
        total = total + rz[k].astype(jnp.float32)
    ids = g * 16 + lax.broadcasted_iota(jnp.int32, total.shape, 0)
    fin[...] = jnp.where(ids < length, own_rows[...] + total, 0.0).astype(jnp.bfloat16)
    push(fin, fin_in, BACK, BACK, sibling)
    out[d] = jnp.where(busy == d, fin[...].astype(jnp.float32), 0.0).astype(jnp.bfloat16)
    take(fin_in, BACK)
    out[1 - d] = jnp.where(busy == d, fin_in[...].astype(jnp.float32), 0.0).astype(jnp.bfloat16)
    for copy in started:
        copy.wait_send()


def fused(hidden_in, span_lengths, norm_gain, query_weight, key_weight, value_weight, out_weight):
    _, rows, width = hidden_in.shape
    head_size = query_weight.shape[1]
    span = rows * 16
    hbm = pl.BlockSpec(memory_space=pltpu.HBM)
    bf16, f32 = jnp.bfloat16, jnp.float32
    wide_table, tall_table = tables(span, head_size)
    return pl.pallas_call(
        span_kernel,
        out_shape=jax.ShapeDtypeStruct(hidden_in.shape, bf16),
        in_specs=[pl.BlockSpec(memory_space=pltpu.SMEM)] + [hbm] * 8,
        out_specs=pl.BlockSpec(memory_space=pltpu.VMEM),
        scratch_shapes=[
            pltpu.VMEM((width,), bf16),
            pltpu.VMEM((rows, width), bf16),
            pltpu.VMEM((rows, width), bf16),
            pltpu.VMEM((rows, width), f32),
            pltpu.VMEM((8, rows, width), bf16),
            pltpu.VMEM((2, width, head_size), bf16),
            pltpu.VMEM((4 * key_weight.shape[1], width), bf16),
            pltpu.VMEM((2 * head_size, width), bf16),
            pltpu.VMEM(wide_table.shape, f32),
            pltpu.VMEM(tall_table.shape, f32),
            pltpu.VMEM((span, head_size), bf16),
            pltpu.VMEM((2, 8, 32, 128), bf16),
            pltpu.VMEM((span // 2, 2 * head_size), bf16),
            pltpu.VMEM((4, rows, width), f32),
            pltpu.VMEM((8, rows, width), bf16),
            pltpu.VMEM((4, rows, width), bf16),
            pltpu.VMEM((4, rows, width), bf16),
            pltpu.VMEM((rows, width), bf16),
            pltpu.VMEM((rows, width), bf16),
            pltpu.SemaphoreType.DMA((COUNT,)),
            pltpu.SemaphoreType.DMA((COUNT,)),
            pltpu.SemaphoreType.DMA((8,)),
        ],
        compiler_params=pltpu.CompilerParams(
            collective_id=0, has_side_effects=True, vmem_limit_bytes=56 * 1024 * 1024
        ),
        cost_estimate=pl.CostEstimate(
            flops=4 * span * width * head_size, bytes_accessed=4 * width * head_size, transcendentals=span * span
        ),
    )(
        span_lengths, hidden_in, norm_gain, query_weight, key_weight.T, value_weight.T,
        out_weight, wide_table, tall_table,
    )


def shards(hidden_in, span_lengths, norm_gain, query_weight, key_weight, value_weight, out_weight):
    slots = hidden_in.shape[0]
    if (
        lax.axis_size("group") == 16
        and lax.axis_size("dp") == 2
        and hidden_in.shape[:2] == (2, 16)
        and query_weight.shape[1] == 128
        and key_weight.shape[1] == 16
    ):
        return fused(
            hidden_in, span_lengths, norm_gain, query_weight, key_weight, value_weight, out_weight
        )
    dp_index = lax.axis_index("dp")
    own_lengths = lax.dynamic_slice_in_dim(span_lengths, dp_index * slots, slots)
    return attend(
        hidden_in, own_lengths, norm_gain, query_weight, key_weight, value_weight, out_weight
    )


def solution(mesh):
    placed = (
        P(("parts", "dp"), "group", None),
        P("parts"),
        P(),
        P(None, "group"),
        P(None, "group"),
        P(None, "group"),
        P("group", None),
    )
    return jax.shard_map(
        shards,
        mesh=mesh,
        in_specs=placed,
        out_specs=P(("parts", "dp"), "group", None),
        check_vma=False,
    )
```

```python
import math

import jax
import jax.numpy as jnp
import numpy as np
from jax import lax
from jax.experimental import pallas as pl
from jax.experimental.pallas import tpu as pltpu
from jax.sharding import PartitionSpec as P

MESH = pl.DeviceIdType.MESH


def partner_2(block, axis, stride):
    count = lax.axis_size(axis)
    route = []
    for low in range(count):
        high = low | 1 << stride
        if high != low and high < count:
            route += [(low, high), (high, low)]
    return lax.ppermute(block, axis, route)


def rms_rows(rows, gain):
    wide = rows.astype(jnp.float32)
    scale = lax.rsqrt(jnp.mean(wide * wide, axis=-1, keepdims=True) + 1e-05)
    return (wide * scale * gain.astype(jnp.float32)).astype(jnp.bfloat16)


def rotate(block):
    count = block.shape[-2]
    width = block.shape[-1]
    half = width // 2
    positions = jnp.arange(count, dtype=jnp.float32)
    freqs = jnp.exp(-math.log(500000.0) * 2.0 * jnp.arange(half, dtype=jnp.float32) / width)
    angles = positions[:, None] * freqs[None, :]
    cosine = jnp.cos(angles)
    sine = jnp.sin(angles)
    first = block[..., :half]
    second = block[..., half:]
    return jnp.concatenate(
        [first * cosine - second * sine, second * cosine + first * sine], axis=-1
    )


def attend(span_rows, lengths, norm_gain, query_weight, key_weight, value_weight, out_weight):
    count, rows, width = span_rows.shape
    groups = lax.axis_size("group")
    span = rows * groups
    head_size = query_weight.shape[1]
    key_cols = key_weight.shape[1]
    normed = rms_rows(span_rows, norm_gain)
    joined = jnp.concatenate([query_weight, key_weight, value_weight], axis=1)
    projected = jnp.einsum(
        "prd,dc->prc",
        lax.all_gather(normed, "group", axis=1, tiled=True),
        joined,
        preferred_element_type=jnp.float32,
    ).astype(jnp.bfloat16)
    query = rotate(projected[..., :head_size].astype(jnp.float32)).astype(jnp.bfloat16)
    key_stack = jnp.swapaxes(projected[..., head_size : head_size + key_cols], 1, 2)
    value_stack = jnp.swapaxes(projected[..., head_size + key_cols :], 1, 2)
    my_index = lax.axis_index("group")
    levels = (head_size // key_cols).bit_length() - 1
    for level in range(levels):
        partner = partner_2((key_stack, value_stack), "group", level)
        first_half = my_index // (1 << level) % 2 == 0
        key_stack = jnp.where(
            first_half,
            jnp.concatenate([key_stack, partner[0]], axis=1),
            jnp.concatenate([partner[0], key_stack], axis=1),
        )
        value_stack = jnp.where(
            first_half,
            jnp.concatenate([value_stack, partner[1]], axis=1),
            jnp.concatenate([partner[1], value_stack], axis=1),
        )
    keys = rotate(jnp.swapaxes(key_stack, 1, 2).astype(jnp.float32)).astype(jnp.bfloat16)
    scores = jnp.einsum(
        "pqd,pkd->pqk", query, keys, preferred_element_type=jnp.float32
    ) / math.sqrt(head_size)
    qpos = jnp.arange(span, dtype=jnp.int32)[None, :, None]
    kpos = jnp.arange(span, dtype=jnp.int32)[None, None, :]
    allowed = kpos <= qpos
    scores = jnp.where(allowed, scores, -1e30)
    peak = jnp.max(scores, axis=-1, keepdims=True)
    expo = jnp.exp(scores - peak)
    weights = (expo / jnp.sum(expo, axis=-1, keepdims=True)).astype(jnp.bfloat16)
    heads_out = jnp.einsum(
        "pqk,pdk->pqd", weights, value_stack, preferred_element_type=jnp.float32
    ).astype(jnp.bfloat16)
    head_rows = jnp.swapaxes(heads_out, 0, 1).reshape(span * count, head_size)
    mixed = lax.psum_scatter(
        jnp.dot(head_rows, out_weight, preferred_element_type=jnp.float32),
        "group",
        scatter_dimension=0,
        tiled=True,
    )
    mixed = jnp.swapaxes(mixed.reshape(rows, count, width), 0, 1)
    row_ids = my_index * rows + jnp.arange(rows, dtype=jnp.int32)
    live = row_ids[None, :] < lengths[:, None]
    return jnp.where(live[..., None], span_rows.astype(jnp.float32) + mixed, 0.0).astype(
        jnp.bfloat16
    )


def slot_positions(count):
    at = np.arange(count)
    return (at // 16 % 4) * 64 + (at // 64) * 16 + at % 16


def tables(span, width):
    half = width // 2
    freqs = 500000.0 ** (-2.0 * np.arange(half) / width)
    angles = slot_positions(span)[:, None] * freqs[None, :]
    cosine, sine = np.cos(angles), np.sin(angles)
    wide_cos = np.concatenate([cosine, cosine], axis=1).astype(np.float32)
    wide_sin = np.concatenate([-sine, sine], axis=1).astype(np.float32)
    return np.stack([wide_cos, wide_sin])


SWAP, GZ, KV, RZ, BACK, FROM_X, FROM_Y, CROSS_X, CROSS_Y, SHARE, COUNT = 0, 1, 5, 13, 17, 18, 22, 26, 30, 34, 46


def span_kernel(
    lens, hidden, gain, wq, wk, wv, wo, table, out,
    gain_rows, own_in, swap_buf, own_rows, x, wqv, wkv, wov, turn, query, kv, heads, part, out_send, rz, fin, fin_in, send, recv, local,
):
    d = lax.axis_index("dp")
    g = lax.axis_index("group")
    z, c = g // 4, g % 4
    zs = (z, z + 1 - 2 * (z % 2), (z + 2) % 4, 3 - z)
    cs = (c, c + 1 - 2 * (c % 2), (c + 2) % 4, 3 - c)
    wide = x.shape[2]

    def chip(zk, ck):
        return {"group": zs[zk] * 4 + cs[ck]}

    near_x, near_y = chip(0, 1), chip(0, 2)
    sibling = {"dp": 1 - d}
    kv_peers = [(k // 4, k % 4) for k in range(1, 8)]
    greeted = [sibling] + [chip(*peer) for peer in kv_peers] + [chip(2, 0), chip(3, 0)]

    early = [
        pltpu.make_async_copy(hidden.at[d], own_in, local.at[6]),
        pltpu.make_async_copy(gain, gain_rows, local.at[7]),
    ]
    loads = [
        pltpu.make_async_copy(wk, wkv.at[pl.ds(c * 16, 16)], local.at[0]),
        pltpu.make_async_copy(wv, wkv.at[pl.ds(64 + c * 16, 16)], local.at[1]),
        pltpu.make_async_copy(wq, wqv.at[c], local.at[2]),
        pltpu.make_async_copy(wo, wov.at[pl.ds(c * 128, 128)], local.at[3]),
        pltpu.make_async_copy(table, turn, local.at[4]),
    ]
    for load in early + loads:
        load.start()

    barrier = pltpu.get_barrier_semaphore()
    for device in greeted:
        pl.semaphore_signal(barrier, inc=1, device_id=device, device_id_type=MESH)
    pl.semaphore_wait(barrier, len(greeted))

    started = []

    def push(source, target, sent, received, device):
        copy = pltpu.make_async_remote_copy(
            src_ref=source, dst_ref=target, send_sem=send.at[sent], recv_sem=recv.at[received],
            device_id=device, device_id_type=MESH,
        )
        copy.start()
        started.append(copy)

    def take(target, received):
        pltpu.make_async_remote_copy(
            src_ref=target, dst_ref=target, send_sem=send.at[received], recv_sem=recv.at[received],
            device_id=sibling, device_id_type=MESH,
        ).wait_recv()

    push(hidden.at[1 - d], swap_buf, SWAP, SWAP, sibling)

    deep = wide // 2

    def piece(which, ck, core, low=0, count=2):
        quarter = deep // 2
        if which == 0:
            return wqv.at[cs[ck], pl.ds(core * deep + low * quarter, count * quarter)]
        if which == 3:
            return wov.at[pl.ds(cs[ck] * 128 + core * 64 + low * 32, count * 32)]
        return wkv.at[pl.ds((which - 1) * 64 + cs[ck] * 16, 16), pl.ds(core * deep, deep)]

    sources = (
        wq.at[pl.ds(d * deep, deep)], wk.at[:, pl.ds(d * deep, deep)], wv.at[:, pl.ds(d * deep, deep)],
        wo.at[pl.ds(d * 64, 64)],
    )

    def give(which):
        push(sources[which], piece(which, 0, d), FROM_X + which, FROM_X + which, near_x)
        push(sources[which], piece(which, 0, d), FROM_Y + which, FROM_Y + which, near_y)

    def share(which, ck):
        index = SHARE + (ck - 1) * 4 + which
        push(piece(which, ck, d), piece(which, ck, d), index, index, sibling)

    def pass_on(which):
        take(piece(which, 1, d), FROM_X + which)
        push(piece(which, 1, d, 0, 1), piece(which, 1, d, 0, 1), CROSS_X + which, CROSS_X + which, near_y)
        take(piece(which, 2, d), FROM_Y + which)
        push(piece(which, 2, d, 1, 1), piece(which, 2, d, 1, 1), CROSS_Y + which, CROSS_Y + which, near_x)
        share(which, 1)
        share(which, 2)

    def across(which):
        take(piece(which, 3, d, 0, 1), CROSS_X + which)
        take(piece(which, 3, d, 1, 1), CROSS_Y + which)
        share(which, 3)

    def shared(which):
        for ck in (1, 2, 3):
            take(piece(which, ck, 1 - d), SHARE + (ck - 1) * 4 + which)

    give(0)
    for which in (1, 2):
        give(which)
        push(sources[which], piece(which, 0, d), CROSS_X + which, CROSS_X + which, chip(0, 3))

    for load in early:
        load.wait()
    busy = jnp.where(lens[0] > 0, 0, 1)
    length = jnp.where(busy == 0, lens[d], lens[2 + d])
    take(swap_buf, SWAP)
    rows = jnp.where(busy == d, own_in[...].astype(jnp.float32), swap_buf[...].astype(jnp.float32))
    own_rows[...] = rows
    scale = lax.rsqrt(jnp.mean(rows * rows, axis=-1, keepdims=True) + 1e-05)

    x[z] = (rows * scale * gain_rows[...].astype(jnp.float32)[None, :]).astype(jnp.bfloat16)

    for k in (3, 2, 1):
        push(x.at[z], x.at[z], GZ + k, GZ + k, chip(k, 0))
    pass_on(0)
    give(3)
    for which in (1, 2):
        take(piece(which, 1, d), FROM_X + which)
        take(piece(which, 2, d), FROM_Y + which)
        take(piece(which, 3, d), CROSS_X + which)
        for ck in (1, 2, 3):
            share(which, ck)
    for load in loads:
        load.wait()
    for k in (1, 2, 3):
        take(x.at[zs[k]], GZ + k)
    shared(1)
    shared(2)

    lines = x[...].reshape(64, wide)
    kv[c, z % 2] = lax.dot_general(
        lines, wkv[...], (((1,), (1,)), ((), ())), preferred_element_type=jnp.float32
    ).astype(jnp.bfloat16)
    own_kv = kv.at[c, z % 2]
    for k, peer in enumerate(kv_peers, 1):
        push(own_kv, own_kv, KV + k, KV + k, chip(*peer))
    across(0)
    shared(0)
    cosine, sine = turn[0, pl.ds(c * 64, 64), :], turn[1, pl.ds(c * 64, 64), :]
    for at in range(4):
        plain = jnp.dot(lines, wqv[at], preferred_element_type=jnp.float32).astype(jnp.bfloat16).astype(jnp.float32)
        query[at * 64 : at * 64 + 64, :] = (plain * cosine + pltpu.roll(plain, 64, 1) * sine).astype(jnp.bfloat16)
    for k, (zk, ck) in enumerate(kv_peers, 1):
        take(kv.at[cs[ck], zs[zk] % 2], KV + k)
    pass_on(3)

    def joined(low):
        return jnp.concatenate([kv[:, half, :, low : low + 64].reshape(256, 64) for half in range(2)], axis=1)

    keys = joined(0).astype(jnp.float32)
    turned = (keys * turn[0] + pltpu.roll(keys, 64, 1) * turn[1]).astype(jnp.bfloat16)
    scores = lax.dot_general(
        query[...], turned, (((1,), (1,)), ((), ())), preferred_element_type=jnp.float32
    ) * (1.0 / math.sqrt(128))

    def position(dim):
        at = lax.broadcasted_iota(jnp.int32, scores.shape, dim)
        return ((at >> 4) & 3) * 64 + (at & 15), at >> 6

    row_at, col_at = position(0)[0] + c * 16, position(1)[0] + position(1)[1] * 16
    scores = jnp.where(col_at <= row_at, scores, -1e30)
    expo = jnp.exp(scores - jnp.max(scores, axis=-1, keepdims=True))
    weights = (expo / jnp.sum(expo, axis=-1, keepdims=True)).astype(jnp.bfloat16)
    mixed = jnp.dot(weights, joined(64), preferred_element_type=jnp.float32).astype(jnp.bfloat16)
    for at in range(4):
        heads[:, at * 128 : at * 128 + 128] = mixed[at * 64 : at * 64 + 64]
    across(3)
    shared(3)

    part[...] = jnp.dot(heads[...], wov[...], preferred_element_type=jnp.float32).reshape(4, 16, wide)
    for k in (2, 3, 1):
        out_send[zs[k]] = part[zs[k]].astype(jnp.bfloat16)
        push(out_send.at[zs[k]], rz.at[k], RZ + k, RZ + k, chip(k, 0))
    total = part[z]
    for k in (2, 3, 1):
        take(rz.at[k], RZ + k)
        total = total + rz[k].astype(jnp.float32)
    ids = g * 16 + lax.broadcasted_iota(jnp.int32, total.shape, 0)
    fin[...] = jnp.where(ids < length, own_rows[...] + total, 0.0).astype(jnp.bfloat16)
    push(fin, fin_in, BACK, BACK, sibling)
    out[d] = jnp.where(busy == d, fin[...].astype(jnp.float32), 0.0).astype(jnp.bfloat16)
    take(fin_in, BACK)
    out[1 - d] = jnp.where(busy == d, fin_in[...].astype(jnp.float32), 0.0).astype(jnp.bfloat16)
    for copy in started:
        copy.wait_send()


def fused(hidden_in, span_lengths, norm_gain, query_weight, key_weight, value_weight, out_weight):
    _, rows, width = hidden_in.shape
    head_size = query_weight.shape[1]
    span = rows * 16
    hbm = pl.BlockSpec(memory_space=pltpu.HBM)
    bf16, f32 = jnp.bfloat16, jnp.float32
    table = tables(span, head_size)
    return pl.pallas_call(
        span_kernel,
        out_shape=jax.ShapeDtypeStruct(hidden_in.shape, bf16),
        in_specs=[pl.BlockSpec(memory_space=pltpu.SMEM)] + [hbm] * 7,
        out_specs=pl.BlockSpec(memory_space=pltpu.VMEM),
        scratch_shapes=[
            pltpu.VMEM((width,), bf16),
            pltpu.VMEM((rows, width), bf16),
            pltpu.VMEM((rows, width), bf16),
            pltpu.VMEM((rows, width), f32),
            pltpu.VMEM((4, rows, width), bf16),
            pltpu.VMEM((4, width, head_size), bf16),
            pltpu.VMEM((8 * key_weight.shape[1], width), bf16),
            pltpu.VMEM((4 * head_size, width), bf16),
            pltpu.VMEM(table.shape, f32),
            pltpu.VMEM((span, head_size), bf16),
            pltpu.VMEM((4, 2, 64, 128), bf16),
            pltpu.VMEM((span // 4, 4 * head_size), bf16),
            pltpu.VMEM((4, rows, width), f32),
            pltpu.VMEM((4, rows, width), bf16),
            pltpu.VMEM((4, rows, width), bf16),
            pltpu.VMEM((rows, width), bf16),
            pltpu.VMEM((rows, width), bf16),
            pltpu.SemaphoreType.DMA((COUNT,)),
            pltpu.SemaphoreType.DMA((COUNT,)),
            pltpu.SemaphoreType.DMA((8,)),
        ],
        compiler_params=pltpu.CompilerParams(
            collective_id=0, has_side_effects=True, vmem_limit_bytes=56 * 1024 * 1024
        ),
        cost_estimate=pl.CostEstimate(
            flops=4 * span * width * head_size, bytes_accessed=4 * width * head_size, transcendentals=span * span
        ),
    )(
        span_lengths, hidden_in, norm_gain, query_weight, key_weight.T, value_weight.T,
        out_weight, table,
    )


def shards(hidden_in, span_lengths, norm_gain, query_weight, key_weight, value_weight, out_weight):
    slots = hidden_in.shape[0]
    if (
        lax.axis_size("group") == 16
        and lax.axis_size("dp") == 2
        and hidden_in.shape[:2] == (2, 16)
        and query_weight.shape[1] == 128
        and key_weight.shape[1] == 16
    ):
        return fused(
            hidden_in, span_lengths, norm_gain, query_weight, key_weight, value_weight, out_weight
        )
    dp_index = lax.axis_index("dp")
    own_lengths = lax.dynamic_slice_in_dim(span_lengths, dp_index * slots, slots)
    return attend(
        hidden_in, own_lengths, norm_gain, query_weight, key_weight, value_weight, out_weight
    )


def solution(mesh):
    placed = (
        P(("parts", "dp"), "group", None),
        P("parts"),
        P(),
        P(None, "group"),
        P(None, "group"),
        P(None, "group"),
        P("group", None),
    )
    return jax.shard_map(
        shards,
        mesh=mesh,
        in_specs=placed,
        out_specs=P(("parts", "dp"), "group", None),
        check_vma=False,
    )
```

```python
import math

import jax
import jax.numpy as jnp
import numpy as np
from jax import lax
from jax.experimental import pallas as pl
from jax.experimental.pallas import tpu as pltpu
from jax.sharding import PartitionSpec as P

MESH = pl.DeviceIdType.MESH


def partner_2(block, axis, stride):
    count = lax.axis_size(axis)
    route = []
    for low in range(count):
        high = low | 1 << stride
        if high != low and high < count:
            route += [(low, high), (high, low)]
    return lax.ppermute(block, axis, route)


def rms_rows(rows, gain):
    wide = rows.astype(jnp.float32)
    scale = lax.rsqrt(jnp.mean(wide * wide, axis=-1, keepdims=True) + 1e-05)
    return (wide * scale * gain.astype(jnp.float32)).astype(jnp.bfloat16)


def rotate(block):
    count = block.shape[-2]
    width = block.shape[-1]
    half = width // 2
    positions = jnp.arange(count, dtype=jnp.float32)
    freqs = jnp.exp(-math.log(500000.0) * 2.0 * jnp.arange(half, dtype=jnp.float32) / width)
    angles = positions[:, None] * freqs[None, :]
    cosine = jnp.cos(angles)
    sine = jnp.sin(angles)
    first = block[..., :half]
    second = block[..., half:]
    return jnp.concatenate(
        [first * cosine - second * sine, second * cosine + first * sine], axis=-1
    )


def attend(span_rows, lengths, norm_gain, query_weight, key_weight, value_weight, out_weight):
    count, rows, width = span_rows.shape
    groups = lax.axis_size("group")
    span = rows * groups
    head_size = query_weight.shape[1]
    key_cols = key_weight.shape[1]
    normed = rms_rows(span_rows, norm_gain)
    joined = jnp.concatenate([query_weight, key_weight, value_weight], axis=1)
    projected = jnp.einsum(
        "prd,dc->prc",
        lax.all_gather(normed, "group", axis=1, tiled=True),
        joined,
        preferred_element_type=jnp.float32,
    ).astype(jnp.bfloat16)
    query = rotate(projected[..., :head_size].astype(jnp.float32)).astype(jnp.bfloat16)
    key_stack = jnp.swapaxes(projected[..., head_size : head_size + key_cols], 1, 2)
    value_stack = jnp.swapaxes(projected[..., head_size + key_cols :], 1, 2)
    my_index = lax.axis_index("group")
    levels = (head_size // key_cols).bit_length() - 1
    for level in range(levels):
        partner = partner_2((key_stack, value_stack), "group", level)
        first_half = my_index // (1 << level) % 2 == 0
        key_stack = jnp.where(
            first_half,
            jnp.concatenate([key_stack, partner[0]], axis=1),
            jnp.concatenate([partner[0], key_stack], axis=1),
        )
        value_stack = jnp.where(
            first_half,
            jnp.concatenate([value_stack, partner[1]], axis=1),
            jnp.concatenate([partner[1], value_stack], axis=1),
        )
    keys = rotate(jnp.swapaxes(key_stack, 1, 2).astype(jnp.float32)).astype(jnp.bfloat16)
    scores = jnp.einsum(
        "pqd,pkd->pqk", query, keys, preferred_element_type=jnp.float32
    ) / math.sqrt(head_size)
    qpos = jnp.arange(span, dtype=jnp.int32)[None, :, None]
    kpos = jnp.arange(span, dtype=jnp.int32)[None, None, :]
    allowed = kpos <= qpos
    scores = jnp.where(allowed, scores, -1e30)
    peak = jnp.max(scores, axis=-1, keepdims=True)
    expo = jnp.exp(scores - peak)
    weights = (expo / jnp.sum(expo, axis=-1, keepdims=True)).astype(jnp.bfloat16)
    heads_out = jnp.einsum(
        "pqk,pdk->pqd", weights, value_stack, preferred_element_type=jnp.float32
    ).astype(jnp.bfloat16)
    head_rows = jnp.swapaxes(heads_out, 0, 1).reshape(span * count, head_size)
    mixed = lax.psum_scatter(
        jnp.dot(head_rows, out_weight, preferred_element_type=jnp.float32),
        "group",
        scatter_dimension=0,
        tiled=True,
    )
    mixed = jnp.swapaxes(mixed.reshape(rows, count, width), 0, 1)
    row_ids = my_index * rows + jnp.arange(rows, dtype=jnp.int32)
    live = row_ids[None, :] < lengths[:, None]
    return jnp.where(live[..., None], span_rows.astype(jnp.float32) + mixed, 0.0).astype(
        jnp.bfloat16
    )


def slot_positions(count):
    at = np.arange(count)
    return (at // 16 % 2) * 128 + (at // 128) * 64 + (at // 32 % 4) * 16 + at % 16


def tables(span, width):
    half = width // 2
    freqs = 500000.0 ** (-2.0 * np.arange(half) / width)
    angles = slot_positions(span)[:, None] * freqs[None, :]
    cosine, sine = np.cos(angles), np.sin(angles)
    wide_cos = np.concatenate([cosine, cosine], axis=1).astype(np.float32)
    wide_sin = np.concatenate([-sine, sine], axis=1).astype(np.float32)
    return np.stack([wide_cos, wide_sin]), np.stack([cosine.T, sine.T]).astype(np.float32)


SWAP, GZ, GX, GY, GD, KV, RD, RX, RY, RZ, BACK, WEIGHT, SHARE, COUNT = 0, 1, 2, 4, 6, 8, 16, 18, 20, 22, 23, 24, 28, 31


def span_kernel(
    lens, hidden, gain, wq, wk, wv, wo, wide_table, tall_table, out,
    gain_rows, own_in, swap_buf, own_rows, x, wqv, wkv, wov, turn_q, turn_k,
    query, kv, heads, part, out_send, rd, rx, ry, rz, fin, fin_in, send, recv, local,
):
    d = lax.axis_index("dp")
    g = lax.axis_index("group")
    z, c = g // 4, g % 4
    plane, mine_z = z % 2, z // 2
    zs = (z, z + 1 - 2 * (z % 2), (z + 2) % 4, 3 - z)
    cs = (c, c + 1 - 2 * (c % 2), (c + 2) % 4, 3 - c)
    wide = x.shape[2]

    def chip(zk, ck):
        return {"group": zs[zk] * 4 + cs[ck]}

    near_x, near_y, partner, far = chip(0, 1), chip(0, 2), chip(1, 0), chip(2, 0)
    sibling = {"dp": 1 - d}
    kv_peers = [(k // 4, k % 4) for k in range(1, 8)]
    greeted = [sibling] + [chip(*peer) for peer in kv_peers] + [far]

    def key_rows(at):
        return wkv.at[pl.ds(at * 32, 16)], wkv.at[pl.ds(at * 32 + 16, 16)]

    def out_rows(at, count=128, low=0):
        return wov.at[pl.ds(at * 128 + low, count)]

    early = [
        pltpu.make_async_copy(hidden.at[d], own_in, local.at[6]),
        pltpu.make_async_copy(gain, gain_rows, local.at[7]),
    ]
    loads = [
        pltpu.make_async_copy(wk, key_rows(plane)[0], local.at[0]),
        pltpu.make_async_copy(wv, key_rows(plane)[1], local.at[1]),
        pltpu.make_async_copy(wq, wqv.at[plane], local.at[2]),
        pltpu.make_async_copy(wo, out_rows(plane), local.at[3]),
        pltpu.make_async_copy(wide_table, turn_q, local.at[4]),
        pltpu.make_async_copy(tall_table, turn_k, local.at[5]),
    ]
    for load in early + loads:
        load.start()

    barrier = pltpu.get_barrier_semaphore()
    for device in greeted:
        pl.semaphore_signal(barrier, inc=1, device_id=device, device_id_type=MESH)
    pl.semaphore_wait(barrier, len(greeted))

    started = []

    def push(source, target, sent, received, device):
        copy = pltpu.make_async_remote_copy(
            src_ref=source, dst_ref=target, send_sem=send.at[sent], recv_sem=recv.at[received],
            device_id=device, device_id_type=MESH,
        )
        copy.start()
        started.append(copy)

    def take(target, received):
        pltpu.make_async_remote_copy(
            src_ref=target, dst_ref=target, send_sem=send.at[received], recv_sem=recv.at[received],
            device_id=sibling, device_id_type=MESH,
        ).wait_recv()

    push(hidden.at[1 - d], swap_buf, SWAP, SWAP, sibling)

    half_q = pl.ds(d * (wide // 2), wide // 2)

    def query_half(at):
        return wqv.at[at, half_q]

    def key_half(at, which):
        return wkv.at[pl.ds(at * 32 + which * 16, 16), half_q]

    def out_half(at):
        return out_rows(at, 64, d * 64)

    push(wq.at[half_q], query_half(plane), WEIGHT, WEIGHT, partner)
    push(wk.at[:, half_q], key_half(plane, 0), WEIGHT + 1, WEIGHT + 1, partner)
    push(wv.at[:, half_q], key_half(plane, 1), WEIGHT + 2, WEIGHT + 2, partner)

    for load in early:
        load.wait()
    busy = jnp.where(lens[0] > 0, 0, 1)
    length = jnp.where(busy == 0, lens[d], lens[2 + d])
    take(swap_buf, SWAP)
    rows = jnp.where(busy == d, own_in[...].astype(jnp.float32), swap_buf[...].astype(jnp.float32))
    own_rows[...] = rows
    scale = lax.rsqrt(jnp.mean(rows * rows, axis=-1, keepdims=True) + 1e-05)

    def slot(ck, k):
        return cs[ck] * 2 + (1 - mine_z if k else mine_z)

    def block(ck, k):
        return x.at[slot(ck, k)]

    x[slot(0, 0)] = (rows * scale * gain_rows[...].astype(jnp.float32)[None, :]).astype(jnp.bfloat16)

    def spread(k):
        push(block(0, k), block(0, k), GX + k, GX + k, near_x)
        push(block(0, k), block(0, k), GY + k, GY + k, near_y)

    push(block(0, 0), block(0, 0), GZ, GZ, far)
    spread(0)
    push(wo.at[pl.ds(d * 64, 64)], out_half(plane), WEIGHT + 3, WEIGHT + 3, partner)
    take(block(0, 1), GZ)
    spread(1)
    take(block(1, 0), GX)
    push(block(1, 0), block(1, 0), GD, GD, near_y)
    take(block(2, 1), GY + 1)
    push(block(2, 1), block(2, 1), GD + 1, GD + 1, near_x)

    other = 1 - plane
    take(query_half(other), WEIGHT)
    push(query_half(other), query_half(other), SHARE, SHARE, sibling)
    take(key_half(other, 0), WEIGHT + 1)
    take(key_half(other, 1), WEIGHT + 2)
    both = wkv.at[pl.ds(other * 32, 32), half_q]
    push(both, both, SHARE + 1, SHARE + 1, sibling)
    for load in loads:
        load.wait()
    rest = pl.ds((1 - d) * (wide // 2), wide // 2)
    take(wqv.at[other, rest], SHARE)
    take(wkv.at[pl.ds(other * 32, 32), rest], SHARE + 1)
    take(block(1, 1), GX + 1)
    take(block(2, 0), GY)
    for k in range(2):
        take(block(3, k), GD + k)

    lines = x[...].reshape(128, wide)
    kv[plane, c] = (
        lax.dot_general(wkv[...], lines, (((1,), (1,)), ((), ())), preferred_element_type=jnp.float32)
        .astype(jnp.bfloat16)
        .reshape(2, 32, 128)
    )
    own_kv = kv.at[plane, c]
    for k, peer in enumerate(kv_peers, 1):
        push(own_kv, own_kv, KV + k, KV + k, chip(*peer))
    turn = (turn_q[0, pl.ds(plane * 128, 128), :], turn_q[1, pl.ds(plane * 128, 128), :])
    for at in range(2):
        plain = jnp.dot(lines, wqv[at], preferred_element_type=jnp.float32).astype(jnp.bfloat16).astype(jnp.float32)
        query[at * 128 : at * 128 + 128, :] = (plain * turn[0] + pltpu.roll(plain, 64, 1) * turn[1]).astype(jnp.bfloat16)
    take(out_half(other), WEIGHT + 3)
    push(out_half(other), out_half(other), SHARE + 2, SHARE + 2, sibling)
    for k, (zk, ck) in enumerate(kv_peers, 1):
        take(kv.at[zs[zk] % 2, cs[ck]], KV + k)

    def joined(low):
        def part_of(half, bit):
            return kv[half, :, bit, low : low + 16, :].reshape(64, 128)

        return jnp.concatenate(
            [jnp.concatenate([part_of(half, 0), part_of(half, 1)], axis=0) for half in range(2)], axis=1
        )

    keys = joined(0).astype(jnp.float32)
    upper, lower = keys[:64], keys[64:]
    turned = jnp.concatenate(
        [upper * turn_k[0] - lower * turn_k[1], lower * turn_k[0] + upper * turn_k[1]], axis=0
    ).astype(jnp.bfloat16)
    scores = jnp.dot(query[...], turned, preferred_element_type=jnp.float32) * (1.0 / math.sqrt(128))

    def position(dim):
        at = lax.broadcasted_iota(jnp.int32, scores.shape, dim)
        return ((at >> 4) & 1) * 128 + ((at >> 5) & 3) * 16 + (at & 15), at >> 7

    row_at, col_at = position(0)[0] + plane * 64, position(1)[0] + position(1)[1] * 64
    scores = jnp.where(col_at <= row_at, scores, -1e30)
    expo = jnp.exp(scores - jnp.max(scores, axis=-1, keepdims=True))
    weights = (expo / jnp.sum(expo, axis=-1, keepdims=True)).astype(jnp.bfloat16)
    mixed = lax.dot_general(
        weights, joined(16), (((1,), (1,)), ((), ())), preferred_element_type=jnp.float32
    ).astype(jnp.bfloat16)
    heads[:, 0:128] = mixed[0:128]
    heads[:, 128:256] = mixed[128:256]
    take(out_rows(other, 64, (1 - d) * 64), SHARE + 2)

    def partial(ck):
        mine = heads[pl.ds(cs[ck] * 32, 32), :]
        return jnp.dot(mine, wov[...], preferred_element_type=jnp.float32).reshape(2, 16, wide)

    out_send[pl.ds(cs[3] * 2, 2)] = partial(3).astype(jnp.bfloat16)
    push(out_send.at[slot(3, 1)], rd.at[1], RD + 1, RD + 1, near_y)
    push(out_send.at[slot(3, 0)], rd.at[0], RD, RD, near_x)
    part[pl.ds(cs[2] * 2, 2)] = partial(2)
    part[pl.ds(cs[1] * 2, 2)] = partial(1)

    def hand_on(ck, k, with_relayed):
        own = part[slot(ck, k)]
        if with_relayed:
            take(rd.at[k], RD + k)
            own = own + rd[k].astype(jnp.float32)
        out_send[slot(ck, k)] = own.astype(jnp.bfloat16)
        if ck == 1:
            push(out_send.at[slot(1, k)], rx.at[k], RX + k, RX + k, near_x)
        else:
            push(out_send.at[slot(2, k)], ry.at[k], RY + k, RY + k, near_y)

    hand_on(2, 1, False)
    hand_on(1, 0, False)
    part[pl.ds(cs[0] * 2, 2)] = partial(0)
    hand_on(1, 1, True)
    hand_on(2, 0, True)

    def column_sum(k):
        take(rx.at[k], RX + k)
        take(ry.at[k], RY + k)
        return part[slot(0, k)] + rx[k].astype(jnp.float32) + ry[k].astype(jnp.float32)

    out_send[slot(0, 1)] = column_sum(1).astype(jnp.bfloat16)
    push(out_send.at[slot(0, 1)], rz, RZ, RZ, far)
    total = column_sum(0)
    take(rz, RZ)
    total = total + rz[...].astype(jnp.float32)
    ids = g * 16 + lax.broadcasted_iota(jnp.int32, total.shape, 0)
    fin[...] = jnp.where(ids < length, own_rows[...] + total, 0.0).astype(jnp.bfloat16)
    push(fin, fin_in, BACK, BACK, sibling)
    out[d] = jnp.where(busy == d, fin[...].astype(jnp.float32), 0.0).astype(jnp.bfloat16)
    take(fin_in, BACK)
    out[1 - d] = jnp.where(busy == d, fin_in[...].astype(jnp.float32), 0.0).astype(jnp.bfloat16)
    for copy in started:
        copy.wait_send()


def fused(hidden_in, span_lengths, norm_gain, query_weight, key_weight, value_weight, out_weight):
    _, rows, width = hidden_in.shape
    head_size = query_weight.shape[1]
    span = rows * 16
    hbm = pl.BlockSpec(memory_space=pltpu.HBM)
    bf16, f32 = jnp.bfloat16, jnp.float32
    wide_table, tall_table = tables(span, head_size)
    return pl.pallas_call(
        span_kernel,
        out_shape=jax.ShapeDtypeStruct(hidden_in.shape, bf16),
        in_specs=[pl.BlockSpec(memory_space=pltpu.SMEM)] + [hbm] * 8,
        out_specs=pl.BlockSpec(memory_space=pltpu.VMEM),
        scratch_shapes=[
            pltpu.VMEM((width,), bf16),
            pltpu.VMEM((rows, width), bf16),
            pltpu.VMEM((rows, width), bf16),
            pltpu.VMEM((rows, width), f32),
            pltpu.VMEM((8, rows, width), bf16),
            pltpu.VMEM((2, width, head_size), bf16),
            pltpu.VMEM((4 * key_weight.shape[1], width), bf16),
            pltpu.VMEM((2 * head_size, width), bf16),
            pltpu.VMEM(wide_table.shape, f32),
            pltpu.VMEM(tall_table.shape, f32),
            pltpu.VMEM((span, head_size), bf16),
            pltpu.VMEM((2, 4, 2, 32, 128), bf16),
            pltpu.VMEM((span // 2, 2 * head_size), bf16),
            pltpu.VMEM((8, rows, width), f32),
            pltpu.VMEM((8, rows, width), bf16),
            pltpu.VMEM((2, rows, width), bf16),
            pltpu.VMEM((2, rows, width), bf16),
            pltpu.VMEM((2, rows, width), bf16),
            pltpu.VMEM((rows, width), bf16),
            pltpu.VMEM((rows, width), bf16),
            pltpu.VMEM((rows, width), bf16),
            pltpu.SemaphoreType.DMA((COUNT,)),
            pltpu.SemaphoreType.DMA((COUNT,)),
            pltpu.SemaphoreType.DMA((8,)),
        ],
        compiler_params=pltpu.CompilerParams(
            collective_id=0, has_side_effects=True, vmem_limit_bytes=56 * 1024 * 1024
        ),
        cost_estimate=pl.CostEstimate(
            flops=4 * span * width * head_size, bytes_accessed=4 * width * head_size, transcendentals=span * span
        ),
    )(
        span_lengths, hidden_in, norm_gain, query_weight, key_weight.T, value_weight.T,
        out_weight, wide_table, tall_table,
    )


def shards(hidden_in, span_lengths, norm_gain, query_weight, key_weight, value_weight, out_weight):
    slots = hidden_in.shape[0]
    if (
        lax.axis_size("group") == 16
        and lax.axis_size("dp") == 2
        and hidden_in.shape[:2] == (2, 16)
        and query_weight.shape[1] == 128
        and key_weight.shape[1] == 16
    ):
        return fused(
            hidden_in, span_lengths, norm_gain, query_weight, key_weight, value_weight, out_weight
        )
    dp_index = lax.axis_index("dp")
    own_lengths = lax.dynamic_slice_in_dim(span_lengths, dp_index * slots, slots)
    return attend(
        hidden_in, own_lengths, norm_gain, query_weight, key_weight, value_weight, out_weight
    )


def solution(mesh):
    placed = (
        P(("parts", "dp"), "group", None),
        P("parts"),
        P(),
        P(None, "group"),
        P(None, "group"),
        P(None, "group"),
        P("group", None),
    )
    return jax.shard_map(
        shards,
        mesh=mesh,
        in_specs=placed,
        out_specs=P(("parts", "dp"), "group", None),
        check_vma=False,
    )
```

```python
import math

import jax
import jax.numpy as jnp
import numpy as np
from jax import lax
from jax.experimental import pallas as pl
from jax.experimental.pallas import tpu as pltpu
from jax.sharding import PartitionSpec as P

MESH = pl.DeviceIdType.MESH


def partner_2(block, axis, stride):
    count = lax.axis_size(axis)
    route = []
    for low in range(count):
        high = low | 1 << stride
        if high != low and high < count:
            route += [(low, high), (high, low)]
    return lax.ppermute(block, axis, route)


def rms_rows(rows, gain):
    wide = rows.astype(jnp.float32)
    scale = lax.rsqrt(jnp.mean(wide * wide, axis=-1, keepdims=True) + 1e-05)
    return (wide * scale * gain.astype(jnp.float32)).astype(jnp.bfloat16)


def rotate(block):
    count = block.shape[-2]
    width = block.shape[-1]
    half = width // 2
    positions = jnp.arange(count, dtype=jnp.float32)
    freqs = jnp.exp(-math.log(500000.0) * 2.0 * jnp.arange(half, dtype=jnp.float32) / width)
    angles = positions[:, None] * freqs[None, :]
    cosine = jnp.cos(angles)
    sine = jnp.sin(angles)
    first = block[..., :half]
    second = block[..., half:]
    return jnp.concatenate(
        [first * cosine - second * sine, second * cosine + first * sine], axis=-1
    )


def attend(span_rows, lengths, norm_gain, query_weight, key_weight, value_weight, out_weight):
    count, rows, width = span_rows.shape
    groups = lax.axis_size("group")
    span = rows * groups
    head_size = query_weight.shape[1]
    key_cols = key_weight.shape[1]
    normed = rms_rows(span_rows, norm_gain)
    joined = jnp.concatenate([query_weight, key_weight, value_weight], axis=1)
    projected = jnp.einsum(
        "prd,dc->prc",
        lax.all_gather(normed, "group", axis=1, tiled=True),
        joined,
        preferred_element_type=jnp.float32,
    ).astype(jnp.bfloat16)
    query = rotate(projected[..., :head_size].astype(jnp.float32)).astype(jnp.bfloat16)
    key_stack = jnp.swapaxes(projected[..., head_size : head_size + key_cols], 1, 2)
    value_stack = jnp.swapaxes(projected[..., head_size + key_cols :], 1, 2)
    my_index = lax.axis_index("group")
    levels = (head_size // key_cols).bit_length() - 1
    for level in range(levels):
        partner = partner_2((key_stack, value_stack), "group", level)
        first_half = my_index // (1 << level) % 2 == 0
        key_stack = jnp.where(
            first_half,
            jnp.concatenate([key_stack, partner[0]], axis=1),
            jnp.concatenate([partner[0], key_stack], axis=1),
        )
        value_stack = jnp.where(
            first_half,
            jnp.concatenate([value_stack, partner[1]], axis=1),
            jnp.concatenate([partner[1], value_stack], axis=1),
        )
    keys = rotate(jnp.swapaxes(key_stack, 1, 2).astype(jnp.float32)).astype(jnp.bfloat16)
    scores = jnp.einsum(
        "pqd,pkd->pqk", query, keys, preferred_element_type=jnp.float32
    ) / math.sqrt(head_size)
    qpos = jnp.arange(span, dtype=jnp.int32)[None, :, None]
    kpos = jnp.arange(span, dtype=jnp.int32)[None, None, :]
    allowed = kpos <= qpos
    scores = jnp.where(allowed, scores, -1e30)
    peak = jnp.max(scores, axis=-1, keepdims=True)
    expo = jnp.exp(scores - peak)
    weights = (expo / jnp.sum(expo, axis=-1, keepdims=True)).astype(jnp.bfloat16)
    heads_out = jnp.einsum(
        "pqk,pdk->pqd", weights, value_stack, preferred_element_type=jnp.float32
    ).astype(jnp.bfloat16)
    head_rows = jnp.swapaxes(heads_out, 0, 1).reshape(span * count, head_size)
    mixed = lax.psum_scatter(
        jnp.dot(head_rows, out_weight, preferred_element_type=jnp.float32),
        "group",
        scatter_dimension=0,
        tiled=True,
    )
    mixed = jnp.swapaxes(mixed.reshape(rows, count, width), 0, 1)
    row_ids = my_index * rows + jnp.arange(rows, dtype=jnp.int32)
    live = row_ids[None, :] < lengths[:, None]
    return jnp.where(live[..., None], span_rows.astype(jnp.float32) + mixed, 0.0).astype(
        jnp.bfloat16
    )


def slot_positions(count):
    at = np.arange(count)
    return (at // 16 % 2) * 128 + (at // 128) * 64 + (at // 32 % 4) * 16 + at % 16


def tables(span, width):
    half = width // 2
    freqs = 500000.0 ** (-2.0 * np.arange(half) / width)
    angles = slot_positions(span)[:, None] * freqs[None, :]
    cosine, sine = np.cos(angles), np.sin(angles)
    wide_cos = np.concatenate([cosine, cosine], axis=1).astype(np.float32)
    wide_sin = np.concatenate([-sine, sine], axis=1).astype(np.float32)
    return np.stack([wide_cos, wide_sin]), np.stack([cosine.T, sine.T]).astype(np.float32)


SWAP, GZ, GX, GY, GD, KV, RD, RX, RY, RZ, BACK, WEIGHT, SHARE, COUNT = 0, 1, 2, 4, 6, 8, 16, 18, 20, 22, 23, 24, 28, 31


def span_kernel(
    lens, hidden, gain, wq, wk, wv, wo, wide_table, tall_table, out,
    gain_rows, own_in, swap_buf, own_rows, x, wqv, wkv, wov, turn_q, turn_k,
    query, kv, heads, part, out_send, rd, rx, ry, rz, fin, fin_in, send, recv, local,
):
    d = lax.axis_index("dp")
    g = lax.axis_index("group")
    z, c = g // 4, g % 4
    plane, mine_z = z % 2, z // 2
    zs = (z, z + 1 - 2 * (z % 2), (z + 2) % 4, 3 - z)
    cs = (c, c + 1 - 2 * (c % 2), (c + 2) % 4, 3 - c)
    wide = x.shape[2]

    def chip(zk, ck):
        return {"group": zs[zk] * 4 + cs[ck]}

    near_x, near_y, partner, far = chip(0, 1), chip(0, 2), chip(1, 0), chip(2, 0)
    sibling = {"dp": 1 - d}
    kv_peers = [(k // 4, k % 4) for k in range(1, 8)]
    greeted = [sibling] + [chip(*peer) for peer in kv_peers] + [far]

    def key_rows(at):
        return wkv.at[pl.ds(at * 32, 16)], wkv.at[pl.ds(at * 32 + 16, 16)]

    def out_rows(at, count=128, low=0):
        return wov.at[pl.ds(at * 128 + low, count)]

    early = [
        pltpu.make_async_copy(hidden.at[d], own_in, local.at[6]),
        pltpu.make_async_copy(gain, gain_rows, local.at[7]),
    ]
    loads = [
        pltpu.make_async_copy(wk, key_rows(plane)[0], local.at[0]),
        pltpu.make_async_copy(wv, key_rows(plane)[1], local.at[1]),
        pltpu.make_async_copy(wq, wqv.at[plane], local.at[2]),
        pltpu.make_async_copy(wo, out_rows(plane), local.at[3]),
        pltpu.make_async_copy(wide_table, turn_q, local.at[4]),
        pltpu.make_async_copy(tall_table, turn_k, local.at[5]),
    ]
    for load in early + loads:
        load.start()

    barrier = pltpu.get_barrier_semaphore()
    for device in greeted:
        pl.semaphore_signal(barrier, inc=1, device_id=device, device_id_type=MESH)
    pl.semaphore_wait(barrier, len(greeted))

    started = []

    def push(source, target, sent, received, device):
        copy = pltpu.make_async_remote_copy(
            src_ref=source, dst_ref=target, send_sem=send.at[sent], recv_sem=recv.at[received],
            device_id=device, device_id_type=MESH,
        )
        copy.start()
        started.append(copy)

    def take(target, received):
        pltpu.make_async_remote_copy(
            src_ref=target, dst_ref=target, send_sem=send.at[received], recv_sem=recv.at[received],
            device_id=sibling, device_id_type=MESH,
        ).wait_recv()

    push(hidden.at[1 - d], swap_buf, SWAP, SWAP, sibling)

    half_q = pl.ds(d * (wide // 2), wide // 2)

    def query_half(at):
        return wqv.at[at, half_q]

    def key_half(at, which):
        return wkv.at[pl.ds(at * 32 + which * 16, 16), half_q]

    def out_half(at):
        return out_rows(at, 64, d * 64)

    for load in early:
        load.wait()
    busy = jnp.where(lens[0] > 0, 0, 1)
    length = jnp.where(busy == 0, lens[d], lens[2 + d])
    take(swap_buf, SWAP)
    rows = jnp.where(busy == d, own_in[...].astype(jnp.float32), swap_buf[...].astype(jnp.float32))
    own_rows[...] = rows
    scale = lax.rsqrt(jnp.mean(rows * rows, axis=-1, keepdims=True) + 1e-05)

    def slot(ck, k):
        return cs[ck] * 2 + (1 - mine_z if k else mine_z)

    def block(ck, k):
        return x.at[slot(ck, k)]

    x[slot(0, 0)] = (rows * scale * gain_rows[...].astype(jnp.float32)[None, :]).astype(jnp.bfloat16)

    def spread(k):
        push(block(0, k), block(0, k), GX + k, GX + k, near_x)
        push(block(0, k), block(0, k), GY + k, GY + k, near_y)

    push(block(0, 0), block(0, 0), GZ, GZ, far)
    spread(0)
    push(wq.at[half_q], query_half(plane), WEIGHT, WEIGHT, partner)
    push(wk.at[:, half_q], key_half(plane, 0), WEIGHT + 1, WEIGHT + 1, partner)
    push(wv.at[:, half_q], key_half(plane, 1), WEIGHT + 2, WEIGHT + 2, partner)
    push(wo.at[pl.ds(d * 64, 64)], out_half(plane), WEIGHT + 3, WEIGHT + 3, partner)
    take(block(0, 1), GZ)
    spread(1)
    take(block(1, 0), GX)
    push(block(1, 0), block(1, 0), GD, GD, near_y)
    take(block(2, 1), GY + 1)
    push(block(2, 1), block(2, 1), GD + 1, GD + 1, near_x)

    other = 1 - plane
    take(query_half(other), WEIGHT)
    push(query_half(other), query_half(other), SHARE, SHARE, sibling)
    take(key_half(other, 0), WEIGHT + 1)
    take(key_half(other, 1), WEIGHT + 2)
    both = wkv.at[pl.ds(other * 32, 32), half_q]
    push(both, both, SHARE + 1, SHARE + 1, sibling)
    for load in loads:
        load.wait()
    rest = pl.ds((1 - d) * (wide // 2), wide // 2)
    take(wqv.at[other, rest], SHARE)
    take(wkv.at[pl.ds(other * 32, 32), rest], SHARE + 1)
    take(block(1, 1), GX + 1)
    take(block(2, 0), GY)
    for k in range(2):
        take(block(3, k), GD + k)

    lines = x[...].reshape(128, wide)
    kv[plane, c] = (
        lax.dot_general(wkv[...], lines, (((1,), (1,)), ((), ())), preferred_element_type=jnp.float32)
        .astype(jnp.bfloat16)
        .reshape(2, 32, 128)
    )
    own_kv = kv.at[plane, c]
    for k, peer in enumerate(kv_peers, 1):
        push(own_kv, own_kv, KV + k, KV + k, chip(*peer))
    turn = (turn_q[0, pl.ds(plane * 128, 128), :], turn_q[1, pl.ds(plane * 128, 128), :])
    for at in range(2):
        plain = jnp.dot(lines, wqv[at], preferred_element_type=jnp.float32).astype(jnp.bfloat16).astype(jnp.float32)
        query[at * 128 : at * 128 + 128, :] = (plain * turn[0] + pltpu.roll(plain, 64, 1) * turn[1]).astype(jnp.bfloat16)
    take(out_half(other), WEIGHT + 3)
    push(out_half(other), out_half(other), SHARE + 2, SHARE + 2, sibling)
    for k, (zk, ck) in enumerate(kv_peers, 1):
        take(kv.at[zs[zk] % 2, cs[ck]], KV + k)

    def joined(low):
        def part_of(half, bit):
            return kv[half, :, bit, low : low + 16, :].reshape(64, 128)

        return jnp.concatenate(
            [jnp.concatenate([part_of(half, 0), part_of(half, 1)], axis=0) for half in range(2)], axis=1
        )

    keys = joined(0).astype(jnp.float32)
    upper, lower = keys[:64], keys[64:]
    turned = jnp.concatenate(
        [upper * turn_k[0] - lower * turn_k[1], lower * turn_k[0] + upper * turn_k[1]], axis=0
    ).astype(jnp.bfloat16)
    scores = jnp.dot(query[...], turned, preferred_element_type=jnp.float32) * (1.0 / math.sqrt(128))

    def position(dim):
        at = lax.broadcasted_iota(jnp.int32, scores.shape, dim)
        return ((at >> 4) & 1) * 128 + ((at >> 5) & 3) * 16 + (at & 15), at >> 7

    row_at, col_at = position(0)[0] + plane * 64, position(1)[0] + position(1)[1] * 64
    scores = jnp.where(col_at <= row_at, scores, -1e30)
    expo = jnp.exp(scores - jnp.max(scores, axis=-1, keepdims=True))
    weights = (expo / jnp.sum(expo, axis=-1, keepdims=True)).astype(jnp.bfloat16)
    mixed = lax.dot_general(
        weights, joined(16), (((1,), (1,)), ((), ())), preferred_element_type=jnp.float32
    ).astype(jnp.bfloat16)
    heads[:, 0:128] = mixed[0:128]
    heads[:, 128:256] = mixed[128:256]
    take(out_rows(other, 64, (1 - d) * 64), SHARE + 2)

    def partial(ck):
        mine = heads[pl.ds(cs[ck] * 32, 32), :]
        return jnp.dot(mine, wov[...], preferred_element_type=jnp.float32).reshape(2, 16, wide)

    out_send[pl.ds(cs[3] * 2, 2)] = partial(3).astype(jnp.bfloat16)
    push(out_send.at[slot(3, 1)], rd.at[1], RD + 1, RD + 1, near_y)
    push(out_send.at[slot(3, 0)], rd.at[0], RD, RD, near_x)
    part[pl.ds(cs[2] * 2, 2)] = partial(2)
    part[pl.ds(cs[1] * 2, 2)] = partial(1)

    def hand_on(ck, k, with_relayed):
        own = part[slot(ck, k)]
        if with_relayed:
            take(rd.at[k], RD + k)
            own = own + rd[k].astype(jnp.float32)
        out_send[slot(ck, k)] = own.astype(jnp.bfloat16)
        if ck == 1:
            push(out_send.at[slot(1, k)], rx.at[k], RX + k, RX + k, near_x)
        else:
            push(out_send.at[slot(2, k)], ry.at[k], RY + k, RY + k, near_y)

    hand_on(2, 1, False)
    hand_on(1, 0, False)
    part[pl.ds(cs[0] * 2, 2)] = partial(0)
    hand_on(1, 1, True)
    hand_on(2, 0, True)

    def column_sum(k):
        take(rx.at[k], RX + k)
        take(ry.at[k], RY + k)
        return part[slot(0, k)] + rx[k].astype(jnp.float32) + ry[k].astype(jnp.float32)

    out_send[slot(0, 1)] = column_sum(1).astype(jnp.bfloat16)
    push(out_send.at[slot(0, 1)], rz, RZ, RZ, far)
    total = column_sum(0)
    take(rz, RZ)
    total = total + rz[...].astype(jnp.float32)
    ids = g * 16 + lax.broadcasted_iota(jnp.int32, total.shape, 0)
    fin[...] = jnp.where(ids < length, own_rows[...] + total, 0.0).astype(jnp.bfloat16)
    push(fin, fin_in, BACK, BACK, sibling)
    out[d] = jnp.where(busy == d, fin[...].astype(jnp.float32), 0.0).astype(jnp.bfloat16)
    take(fin_in, BACK)
    out[1 - d] = jnp.where(busy == d, fin_in[...].astype(jnp.float32), 0.0).astype(jnp.bfloat16)
    for copy in started:
        copy.wait_send()


def fused(hidden_in, span_lengths, norm_gain, query_weight, key_weight, value_weight, out_weight):
    _, rows, width = hidden_in.shape
    head_size = query_weight.shape[1]
    span = rows * 16
    hbm = pl.BlockSpec(memory_space=pltpu.HBM)
    bf16, f32 = jnp.bfloat16, jnp.float32
    wide_table, tall_table = tables(span, head_size)
    return pl.pallas_call(
        span_kernel,
        out_shape=jax.ShapeDtypeStruct(hidden_in.shape, bf16),
        in_specs=[pl.BlockSpec(memory_space=pltpu.SMEM)] + [hbm] * 8,
        out_specs=pl.BlockSpec(memory_space=pltpu.VMEM),
        scratch_shapes=[
            pltpu.VMEM((width,), bf16),
            pltpu.VMEM((rows, width), bf16),
            pltpu.VMEM((rows, width), bf16),
            pltpu.VMEM((rows, width), f32),
            pltpu.VMEM((8, rows, width), bf16),
            pltpu.VMEM((2, width, head_size), bf16),
            pltpu.VMEM((4 * key_weight.shape[1], width), bf16),
            pltpu.VMEM((2 * head_size, width), bf16),
            pltpu.VMEM(wide_table.shape, f32),
            pltpu.VMEM(tall_table.shape, f32),
            pltpu.VMEM((span, head_size), bf16),
            pltpu.VMEM((2, 4, 2, 32, 128), bf16),
            pltpu.VMEM((span // 2, 2 * head_size), bf16),
            pltpu.VMEM((8, rows, width), f32),
            pltpu.VMEM((8, rows, width), bf16),
            pltpu.VMEM((2, rows, width), bf16),
            pltpu.VMEM((2, rows, width), bf16),
            pltpu.VMEM((2, rows, width), bf16),
            pltpu.VMEM((rows, width), bf16),
            pltpu.VMEM((rows, width), bf16),
            pltpu.VMEM((rows, width), bf16),
            pltpu.SemaphoreType.DMA((COUNT,)),
            pltpu.SemaphoreType.DMA((COUNT,)),
            pltpu.SemaphoreType.DMA((8,)),
        ],
        compiler_params=pltpu.CompilerParams(
            collective_id=0, has_side_effects=True, vmem_limit_bytes=56 * 1024 * 1024
        ),
        cost_estimate=pl.CostEstimate(
            flops=4 * span * width * head_size, bytes_accessed=4 * width * head_size, transcendentals=span * span
        ),
    )(
        span_lengths, hidden_in, norm_gain, query_weight, key_weight.T, value_weight.T,
        out_weight, wide_table, tall_table,
    )


def shards(hidden_in, span_lengths, norm_gain, query_weight, key_weight, value_weight, out_weight):
    slots = hidden_in.shape[0]
    if (
        lax.axis_size("group") == 16
        and lax.axis_size("dp") == 2
        and hidden_in.shape[:2] == (2, 16)
        and query_weight.shape[1] == 128
        and key_weight.shape[1] == 16
    ):
        return fused(
            hidden_in, span_lengths, norm_gain, query_weight, key_weight, value_weight, out_weight
        )
    dp_index = lax.axis_index("dp")
    own_lengths = lax.dynamic_slice_in_dim(span_lengths, dp_index * slots, slots)
    return attend(
        hidden_in, own_lengths, norm_gain, query_weight, key_weight, value_weight, out_weight
    )


def solution(mesh):
    placed = (
        P(("parts", "dp"), "group", None),
        P("parts"),
        P(),
        P(None, "group"),
        P(None, "group"),
        P(None, "group"),
        P("group", None),
    )
    return jax.shard_map(
        shards,
        mesh=mesh,
        in_specs=placed,
        out_specs=P(("parts", "dp"), "group", None),
        check_vma=False,
    )
```
